32 devices in a mesh: tasks: 8 (over z, x), group: 4 (over y, core).
Axes of the slice: x: 2, y: 2, z: 4, core: 2. Of those that a mesh axis runs over, the one named last changes fastest.
Arguments:
- support_images: bfloat16 [32, 4, 32, 32, 128], P(('tasks', 'group')), may hold values from -6 to 6
- query_images: bfloat16 [32, 6, 32, 32, 128], P(('tasks', 'group')), may hold values from -6 to 6
- support_target: bfloat16 [32, 4, 8, 8, 128], P(('tasks', 'group')), may hold values from -6 to 6
- query_cotangent: bfloat16 [32, 6, 8, 8, 128], P(('tasks', 'group')), may hold values from -6 to 6
- support_count: int32 [32], P(('tasks', 'group')), may hold values from 1 to 4, as said below
- query_count: int32 [32], P(('tasks', 'group')), may hold values from 1 to 6, as said below
- kernel_one: float32 [3, 3, 128, 128], replicated, may hold values from -0.1875 to 0.1875
- kernel_two: float32 [3, 3, 128, 128], replicated, may hold values from -0.1875 to 0.1875
- gain_one: float32 [128], replicated, may hold values from 0.5 to 1.5
- shift_one: float32 [128], replicated, may hold values from -3 to 3
- gain_two: float32 [128], replicated, may hold values from 0.5 to 1.5
- shift_two: float32 [128], replicated, may hold values from -3 to 3
- outer_one: float32 [128, 128], replicated, as said below
- inner_one: float32 [128, 128], replicated, as said below
- taps_one: float32 [9, 9], replicated, as said below
- outer_two: float32 [128, 128], replicated, as said below
- inner_two: float32 [128, 128], replicated, as said below
- taps_two: float32 [9, 9], replicated, as said below
Outputs:
- query_output: bfloat16 [32, 6, 8, 8, 128], P(('tasks', 'group'))
- support_grad: bfloat16 [32, 4, 32, 32, 128], P(('tasks', 'group'))
- query_grad: bfloat16 [32, 6, 32, 32, 128], P(('tasks', 'group'))
- grad_kernel_one: float32 [3, 3, 128, 128], replicated
- grad_kernel_two: float32 [3, 3, 128, 128], replicated
- grad_gain_one: float32 [128], replicated
- grad_shift_one: float32 [128], replicated
- grad_gain_two: float32 [128], replicated
- grad_shift_two: float32 [128], replicated
- grad_outer_one: float32 [128, 128], replicated
- grad_inner_one: float32 [128, 128], replicated
- grad_taps_one: float32 [9, 9], replicated
- grad_outer_two: float32 [128, 128], replicated
- grad_inner_two: float32 [128, 128], replicated
- grad_taps_two: float32 [9, 9], replicated
The draws below stay inside these ranges and needn't reach their ends.
Inputs may be any that keep to these rules, and one draw needn't show every extreme that they name: Task t uses its first support_count[t] support slots; some task uses all 4. Task t uses its first query_count[t] query slots; some task uses all 6. `outer_one`: the identity plus independent terms. `inner_one`: the identity plus independent terms. `taps_one`: the identity plus independent terms. `outer_two`: the identity plus independent terms. `inner_two`: the identity plus independent terms. `taps_two`: the identity plus independent terms.
All inputs are finite; a program needn't handle non-finite values.
Results may differ from the reference program's by a relative error of at most 0.015.
Values sent between devices are 32-bit elements; how exact they have to be, the bound alone decides.
No kernel may reach another device: no remote copies, remote signals or barrier semaphores. Data moves between devices by JAX's collectives and lax.ppermute only.
A program may use at most 192 MiB of HBM per device.

```python
import math
from functools import partial
import jax
import jax.numpy as jnp
from jax import lax

C = 128
SIDE = 32
S_CAP = 4
Q_CAP = 6
TASKS = 32
OUT = 8


def skewed_counts(key, largest, number):
    draws_one = jax.random.randint(jax.random.fold_in(key, 1), (number,), 1, largest + 1)
    draws_two = jax.random.randint(jax.random.fold_in(key, 2), (number,), 2, largest + 1)
    counts = jnp.minimum(draws_one, draws_two)
    chosen = jax.random.randint(jax.random.fold_in(key, 3), (), 0, number)
    return jnp.where(jnp.arange(number) == chosen, largest, counts).astype(jnp.int32)


def near_identity(key, extent, spread):
    jitter = jax.random.normal(key, (extent, extent), jnp.float32)
    return jnp.eye(extent, dtype=jnp.float32) + jitter * (spread / math.sqrt(extent))


def draw_support_count(key, part):
    key = jax.random.fold_in(key, 5)
    return skewed_counts(key, S_CAP, TASKS)


def draw_query_count(key, part):
    key = jax.random.fold_in(key, 6)
    return skewed_counts(key, Q_CAP, TASKS)


def draw_outer_one(key, part):
    key = jax.random.fold_in(key, 11)
    return near_identity(key, C, 0.5)


def draw_inner_one(key, part):
    key = jax.random.fold_in(key, 12)
    return near_identity(key, C, 0.5)


def draw_taps_one(key, part):
    key = jax.random.fold_in(key, 13)
    return near_identity(key, 9, 0.6)


def draw_outer_two(key, part):
    key = jax.random.fold_in(key, 14)
    return near_identity(key, C, 0.5)


def draw_inner_two(key, part):
    key = jax.random.fold_in(key, 15)
    return near_identity(key, C, 0.5)


def draw_taps_two(key, part):
    key = jax.random.fold_in(key, 16)
    return near_identity(key, 9, 0.6)


def block_scale(rng, shape, pieces, smallest, high):
    def one(position, shards_of):
        heights = jax.random.uniform(jax.random.fold_in(jax.random.fold_in(rng, 6), position), (shards_of,), jnp.float32, smallest / len(pieces), high / len(pieces))
        return jnp.repeat(jnp.exp(heights), shape[position] // shards_of).reshape((-1,) + (1,) * (len(shape) - position - 1))

    level = one(*pieces[0])
    for cut in pieces[1:]:
        level = level * one(*cut)
    return level


def gaussian(own_key, shape, scale, bound, split=(), held_as=jnp.bfloat16):
    values = scale * jax.random.normal(own_key, shape, jnp.float32)
    if split:
        values = values * block_scale(own_key, shape, split, -0.22, 0.18)
    return jnp.clip(values, -bound, bound).astype(held_as)


def setup_inputs(seed: int = 0) -> dict:
    splits = jax.random.split(jax.random.key(seed), 19)
    support_images = gaussian(splits[0], (TASKS, S_CAP, SIDE, SIDE, C), 1.0, 6.0, ((0, 32),))
    query_images = gaussian(splits[1], (TASKS, Q_CAP, SIDE, SIDE, C), 1.0, 6.0, ((0, 32),))
    support_target = gaussian(splits[2], (TASKS, S_CAP, OUT, OUT, C), 1.0, 6.0, ((0, 32),))
    query_cotangent = gaussian(splits[3], (TASKS, Q_CAP, OUT, OUT, C), 1.0, 6.0, ((0, 32),))
    support_count = draw_support_count(jax.random.fold_in(splits[18], 71), 0)
    query_count = draw_query_count(jax.random.fold_in(splits[18], 71), 0)
    kernel_one = gaussian(splits[6], (3, 3, C, C), (9 * C) ** -0.5, 0.1875, (), jnp.float32)
    kernel_two = gaussian(splits[7], (3, 3, C, C), (9 * C) ** -0.5, 0.1875, (), jnp.float32)
    gain_one = jnp.clip(1.0 + 0.1 * jax.random.normal(splits[8], (C,), jnp.float32), 0.5, 1.5)
    shift_one = gaussian(splits[9], (C,), 0.5, 3.0, (), jnp.float32)
    gain_two = jnp.clip(1.0 + 0.1 * jax.random.normal(splits[10], (C,), jnp.float32), 0.5, 1.5)
    shift_two = gaussian(splits[11], (C,), 0.5, 3.0, (), jnp.float32)
    outer_one = draw_outer_one(jax.random.fold_in(splits[18], 71), 0)
    inner_one = draw_inner_one(jax.random.fold_in(splits[18], 71), 0)
    taps_one = draw_taps_one(jax.random.fold_in(splits[18], 71), 0)
    outer_two = draw_outer_two(jax.random.fold_in(splits[18], 71), 0)
    inner_two = draw_inner_two(jax.random.fold_in(splits[18], 71), 0)
    taps_two = draw_taps_two(jax.random.fold_in(splits[18], 71), 0)
    return {"support_images": support_images, "query_images": query_images, "support_target": support_target, "query_cotangent": query_cotangent, "support_count": support_count, "query_count": query_count, "kernel_one": kernel_one, "kernel_two": kernel_two, "gain_one": gain_one, "shift_one": shift_one, "gain_two": gain_two, "shift_two": shift_two, "outer_one": outer_one, "inner_one": inner_one, "taps_one": taps_one, "outer_two": outer_two, "inner_two": inner_two, "taps_two": taps_two}


STEP_RATE = 0.01
PENALTY = 1.0
EPSILON = 1e-05

@jax.custom_vjp
def low(v):
    return lax.optimization_barrier(v.astype(jnp.bfloat16)).astype(jnp.float32)

@jax.custom_vjp
def low_back(v):
    return v

def low_keep(v):
    return (low(v), None)

def low_pass(kept, grad):
    return (grad,)

def back_keep(v):
    return (v, None)

def back_low(kept, grad):
    return (low(grad),)
low.defvjp(low_keep, low_pass)
low_back.defvjp(back_keep, back_low)

def convolve(images, kernel):
    return lax.conv_general_dilated(images, kernel, (1, 1), 'SAME', dimension_numbers=('NHWC', 'HWIO', 'NHWC'), precision=lax.Precision.HIGHEST)

def conv_layer(images, kernel, norm_gain, norm_shift, weights, live_cells):
    raw_out = low_back(convolve(low(images), low(kernel)))
    cell_total = live_cells * raw_out.shape[1] * raw_out.shape[2]
    per_image = weights[:, None, None, None]
    mean_value = lax.optimization_barrier(jnp.sum(raw_out * per_image, axis=(0, 1, 2))) / cell_total
    centred = raw_out - mean_value
    variance = lax.optimization_barrier(jnp.sum(centred * centred * per_image, axis=(0, 1, 2))) / cell_total
    normed = norm_gain * centred * lax.rsqrt(variance + EPSILON) + norm_shift
    active = jax.nn.silu(normed)
    number, height, breadth, channels = active.shape
    return lax.optimization_barrier(jnp.mean(active.reshape(number, height // 2, 2, breadth // 2, 2, channels), axis=(2, 4)))

def network(images, kernel_pair, norms, weights, live_cells):
    hidden = conv_layer(images, kernel_pair[0], norms[0], norms[1], weights, live_cells)
    produced = conv_layer(hidden, kernel_pair[1], norms[2], norms[3], weights, live_cells)
    return produced * weights[:, None, None, None]

def taps_transform(gradient, outer, inner, taps):
    channels = gradient.shape[2]
    flattened = gradient.reshape(9, channels, channels)
    turned = jnp.einsum('gf,fio->gio', taps, flattened, precision=lax.Precision.HIGHEST)
    turned = jnp.einsum('ji,gio->gjo', inner, turned, precision=lax.Precision.HIGHEST)
    turned = jnp.einsum('gjo,po->gjp', turned, outer, precision=lax.Precision.HIGHEST)
    return turned.reshape(3, 3, channels, channels)

def adapted_query(params, support_float, query_float, target_float, support_live, query_live):
    norms = params[2:6]
    factors = params[6:12]
    support_weights = (jnp.arange(support_float.shape[0]) < support_live).astype(jnp.float32)
    query_weights = (jnp.arange(query_float.shape[0]) < query_live).astype(jnp.float32)
    support_cells = support_live.astype(jnp.float32)

    def inner_loss(kernel_pair):
        produced = network(support_float, kernel_pair, norms, support_weights, support_cells)
        return jnp.sum(produced * target_float) / (support_cells * produced.shape[1] * produced.shape[2])
    gradient = jax.grad(inner_loss)((params[0], params[1]))
    fast_one = params[0] - STEP_RATE * taps_transform(gradient[0], factors[0], factors[1], factors[2])
    fast_two = params[1] - STEP_RATE * taps_transform(gradient[1], factors[3], factors[4], factors[5])
    return network(query_float, (fast_one, fast_two), norms, query_weights, query_live.astype(jnp.float32))

def penalty_term(factors):
    return PENALTY * sum((jnp.sum((matrix - jnp.eye(matrix.shape[0], dtype=matrix.dtype)) ** 2) for matrix in factors))

def episode_step(params, running, episode):
    support_images, query_images, support_target, query_cotangent, support_live, query_live = episode
    target_float = support_target.astype(jnp.float32)

    def forward(all_params, support_float, query_float):
        return adapted_query(all_params, support_float, query_float, target_float, support_live, query_live)
    produced, pullback = jax.vjp(forward, params, support_images.astype(jnp.float32), query_images.astype(jnp.float32))
    query_weights = (jnp.arange(query_images.shape[0]) < query_live).astype(jnp.float32)
    seed_grad = query_cotangent.astype(jnp.float32) * query_weights[:, None, None, None] / query_live.astype(jnp.float32)
    param_grads, support_grad, query_grad = pullback(seed_grad)
    running = tuple((total + extra for total, extra in zip(running, param_grads)))
    return (running, (produced.astype(jnp.bfloat16), support_grad.astype(jnp.bfloat16), query_grad.astype(jnp.bfloat16)))

def reference(support_images, query_images, support_target, query_cotangent, support_count, query_count, kernel_one, kernel_two, gain_one, shift_one, gain_two, shift_two, outer_one, inner_one, taps_one, outer_two, inner_two, taps_two):
    params = (kernel_one, kernel_two, gain_one, shift_one, gain_two, shift_two, outer_one, inner_one, taps_one, outer_two, inner_two, taps_two)
    starting = tuple((jnp.zeros_like(param) for param in params))
    totals, produced = lax.scan(partial(episode_step, params), starting, (support_images, query_images, support_target, query_cotangent, support_count, query_count))
    penalty_grads = jax.grad(penalty_term)(params[6:12])
    totals = totals[:6] + tuple((total + extra for total, extra in zip(totals[6:12], penalty_grads)))
    return (produced[0], produced[1], produced[2], totals[0], totals[1], totals[2], totals[3], totals[4], totals[5], totals[6], totals[7], totals[8], totals[9], totals[10], totals[11])
```

```python
from functools import partial

import jax
import jax.numpy as jnp
from jax import lax
from jax.sharding import PartitionSpec as P

STEP_RATE = 0.01
PENALTY = 1.0
EPSILON = 1e-05


def round_value(value):
    return lax.optimization_barrier(value.astype(jnp.bfloat16)).astype(jnp.float32)


def same_value(value):
    return value


def keep_rounded(value):
    return (round_value(value), None)


def pass_grad(kept, grad):
    return (grad,)


def keep_plain(value):
    return (value, None)


def round_grad(kept, grad):
    return (round_value(grad),)


def value_rounder():
    wrapped = jax.custom_vjp(round_value)
    wrapped.defvjp(keep_rounded, pass_grad)
    return wrapped


def grad_rounder():
    wrapped = jax.custom_vjp(same_value)
    wrapped.defvjp(keep_plain, round_grad)
    return wrapped


def convolve(images, kernel):
    return lax.conv_general_dilated(
        images, kernel, (1, 1), "SAME", dimension_numbers=("NHWC", "HWIO", "NHWC")
    )


def conv_layer(images, kernel, norm_gain, norm_shift, weights, live_cells):
    to_bf16 = value_rounder()
    grad_bf16 = grad_rounder()
    raw_out = grad_bf16(convolve(to_bf16(images), to_bf16(kernel)))
    cell_total = live_cells * raw_out.shape[1] * raw_out.shape[2]
    per_image = weights[:, None, None, None]
    mean_value = jnp.sum(raw_out * per_image, axis=(0, 1, 2)) / cell_total
    centred = raw_out - mean_value
    variance = jnp.sum(centred * centred * per_image, axis=(0, 1, 2)) / cell_total
    normed = norm_gain * centred * lax.rsqrt(variance + EPSILON) + norm_shift
    active = jax.nn.silu(normed)
    number, height, breadth, channels = active.shape
    return jnp.mean(active.reshape(number, height // 2, 2, breadth // 2, 2, channels), axis=(2, 4))


def network(images, kernel_pair, norms, weights, live_cells):
    hidden = conv_layer(images, kernel_pair[0], norms[0], norms[1], weights, live_cells)
    produced = conv_layer(hidden, kernel_pair[1], norms[2], norms[3], weights, live_cells)
    return produced * weights[:, None, None, None]


def taps_transform(gradient, outer, inner, taps):
    channels = gradient.shape[2]
    flattened = gradient.reshape(9, channels, channels)
    turned = jnp.einsum("gf,fio->gio", taps, flattened, precision=lax.Precision.HIGHEST)
    turned = jnp.einsum("ji,gio->gjo", inner, turned, precision=lax.Precision.HIGHEST)
    turned = jnp.einsum("gjo,po->gjp", turned, outer, precision=lax.Precision.HIGHEST)
    return turned.reshape(3, 3, channels, channels)


def adapted_query(params, support_float, query_float, target_float, support_live, query_live):
    norms = params[2:6]
    factors = params[6:12]
    support_weights = (jnp.arange(support_float.shape[0]) < support_live).astype(jnp.float32)
    query_weights = (jnp.arange(query_float.shape[0]) < query_live).astype(jnp.float32)
    support_cells = support_live.astype(jnp.float32)

    def inner_loss(kernel_pair):
        produced = network(support_float, kernel_pair, norms, support_weights, support_cells)
        return jnp.sum(produced * target_float) / (
            support_cells * produced.shape[1] * produced.shape[2]
        )

    gradient = jax.grad(inner_loss)((params[0], params[1]))
    fast_one = params[0] - STEP_RATE * taps_transform(
        gradient[0], factors[0], factors[1], factors[2]
    )
    fast_two = params[1] - STEP_RATE * taps_transform(
        gradient[1], factors[3], factors[4], factors[5]
    )
    return network(
        query_float, (fast_one, fast_two), norms, query_weights, query_live.astype(jnp.float32)
    )


def penalty_term(factors):
    return PENALTY * sum(
        (
            jnp.sum((matrix - jnp.eye(matrix.shape[0], dtype=matrix.dtype)) ** 2)
            for matrix in factors
        )
    )


def episode_step(params, running, episode):
    support_images, query_images, support_target, query_cotangent, support_live, query_live = (
        episode
    )
    target_float = support_target.astype(jnp.float32)

    def forward(all_params, support_float, query_float):
        return adapted_query(
            all_params, support_float, query_float, target_float, support_live, query_live
        )

    produced, pullback = jax.vjp(
        forward, params, support_images.astype(jnp.float32), query_images.astype(jnp.float32)
    )
    query_weights = (jnp.arange(query_images.shape[0]) < query_live).astype(jnp.float32)
    seed_grad = (
        query_cotangent.astype(jnp.float32)
        * query_weights[:, None, None, None]
        / query_live.astype(jnp.float32)
    )
    param_grads, support_grad, query_grad = pullback(seed_grad)
    running = tuple((total + extra for total, extra in zip(running, param_grads)))
    return (
        running,
        (
            produced.astype(jnp.bfloat16),
            support_grad.astype(jnp.bfloat16),
            query_grad.astype(jnp.bfloat16),
        ),
    )


def swap_bit(value, axis, bit):
    extent = lax.axis_size(axis)
    return lax.ppermute(value, axis, [(place, place ^ (1 << bit)) for place in range(extent)])


def butterfly_sum(rows, steps, halvings):
    kept = []
    for axis, bit in steps[:halvings]:
        half = rows.shape[0] // 2
        mine = (lax.axis_index(axis) >> bit) & 1
        halves = rows.reshape(2, half, rows.shape[1])
        sent = lax.dynamic_index_in_dim(halves, 1 - mine, 0, keepdims=False)
        held = lax.dynamic_index_in_dim(halves, mine, 0, keepdims=False)
        rows = held + swap_bit(sent, axis, bit)
        kept.append((axis, bit, mine))
    for axis, bit in steps[halvings:]:
        rows = rows + swap_bit(rows, axis, bit)
    for axis, bit, mine in reversed(kept):
        other = swap_bit(rows, axis, bit)
        rows = jnp.concatenate(
            [jnp.where(mine == 0, rows, other), jnp.where(mine == 0, other, rows)], 0
        )
    return rows


def sum_over_mesh(arrays, axes):
    sizes = [lax.axis_size(axis) for axis in axes]
    if any(size & (size - 1) for size in sizes):
        return lax.psum(arrays, axes)
    steps = [(axis, bit) for axis, size in zip(axes, sizes) for bit in range(size.bit_length() - 1)]
    halvings = min(3, len(steps))
    pieces = []
    for array in arrays:
        flat = array.reshape(-1)
        pieces.append(jnp.pad(flat, (0, -flat.size % 128)).reshape(-1, 128))
    counts = [piece.shape[0] for piece in pieces]
    unit = 8 << halvings
    rows = jnp.concatenate(pieces + [jnp.zeros((-sum(counts) % unit, 128), jnp.float32)], 0)
    rows = butterfly_sum(rows, steps, halvings)
    results, start = [], 0
    for array, count in zip(arrays, counts):
        results.append(
            rows[start : start + count].reshape(-1)[: array.size].reshape(array.shape)
        )
        start += count
    return tuple(results)


def body(
    support_images,
    query_images,
    support_target,
    query_cotangent,
    support_count,
    query_count,
    kernel_one,
    kernel_two,
    gain_one,
    shift_one,
    gain_two,
    shift_two,
    outer_one,
    inner_one,
    taps_one,
    outer_two,
    inner_two,
    taps_two,
):
    params = (
        kernel_one,
        kernel_two,
        gain_one,
        shift_one,
        gain_two,
        shift_two,
        outer_one,
        inner_one,
        taps_one,
        outer_two,
        inner_two,
        taps_two,
    )
    starting = tuple((jnp.zeros_like(param) for param in params))
    local_sums, produced = lax.scan(
        partial(episode_step, params),
        starting,
        (support_images, query_images, support_target, query_cotangent, support_count, query_count),
    )
    totals = sum_over_mesh(local_sums, ("group", "tasks"))
    penalty_grads = jax.grad(penalty_term)(params[6:12])
    totals = tuple(totals[:6]) + tuple(
        (total + extra for total, extra in zip(totals[6:12], penalty_grads))
    )
    return (
        produced[0],
        produced[1],
        produced[2],
        totals[0],
        totals[1],
        totals[2],
        totals[3],
        totals[4],
        totals[5],
        totals[6],
        totals[7],
        totals[8],
        totals[9],
        totals[10],
        totals[11],
    )


def solution(mesh):
    return jax.shard_map(
        body,
        mesh=mesh,
        in_specs=(
            P(("tasks", "group"), None, None, None, None),
            P(("tasks", "group"), None, None, None, None),
            P(("tasks", "group"), None, None, None, None),
            P(("tasks", "group"), None, None, None, None),
            P(("tasks", "group")),
            P(("tasks", "group")),
            P(),
            P(),
            P(),
            P(),
            P(),
            P(),
            P(),
            P(),
            P(),
            P(),
            P(),
            P(),
        ),
        out_specs=(
            P(("tasks", "group"), None, None, None, None),
            P(("tasks", "group"), None, None, None, None),
            P(("tasks", "group"), None, None, None, None),
            P(),
            P(),
            P(),
            P(),
            P(),
            P(),
            P(),
            P(),
            P(),
            P(),
            P(),
            P(),
        ),
        check_vma=False,
    )
```

```python
from functools import partial
from types import SimpleNamespace

import jax
import jax.numpy as jnp
from jax import lax
from jax.experimental import pallas as pl
from jax.experimental.pallas import tpu as pltpu
from jax.sharding import PartitionSpec as P

STEP_RATE = 0.01
PENALTY = 1.0
EPSILON = 1e-05
C = 128
F32 = jnp.float32
BF16 = jnp.bfloat16
VMEM_BYTES = 62 << 20
VMEM_SMALL = 24 << 20
AXES = ("tasks", "group")


def shift_down(v):
    place = lax.broadcasted_iota(jnp.int32, v.shape, v.ndim - 2)
    return jnp.where(place == 0, 0.0, pltpu.roll(v, 1, v.ndim - 2))


def shift_up(v):
    place = lax.broadcasted_iota(jnp.int32, v.shape, v.ndim - 2)
    return jnp.where(place == 7, 0.0, pltpu.roll(v, 7, v.ndim - 2))


def put(buf, i, start, m, blocks, v):
    tiles = v.shape[0] // 2

    def store(block, value):
        buf[i, pl.ds(1 + start, tiles), :, C * block : C * block + C] = value.reshape(
            tiles, 16, C
        ).astype(BF16)

    store(1 + m, v)
    if m == 0:
        store(blocks + 1, shift_up(v))
    if m == blocks - 1:
        store(0, shift_down(v))


def put_halo(buf, i, tiles):
    last = buf[i, tiles].astype(F32)
    first = buf[i, 1].astype(F32)
    nothing = jnp.zeros((8, last.shape[1]), F32)
    buf[i, 0] = jnp.concatenate([nothing, last[:8]], 0).astype(BF16)
    buf[i, tiles + 1] = jnp.concatenate([first[8:], nothing], 0).astype(BF16)


def get(ref, i, start, tiles, m):
    return ref[i, pl.ds(start, tiles), :, C * m : C * m + C].reshape(tiles // 2, 2, 2, 8, C)


def set_(ref, i, start, tiles, m, v):
    ref[i, pl.ds(start, tiles), :, C * m : C * m + C] = v.reshape(tiles, 16, C)


def total(v):
    return jnp.sum(v.reshape(-1, 8, C), axis=0)


def channel(v):
    return jnp.broadcast_to(jnp.sum(v, axis=0, keepdims=True), (8, C))


def loop(count, body, carry=0):
    return lax.fori_loop(0, count, body, carry)


def write_weights(dst, tap):
    for r in range(3):
        for j in range(4):
            for o in range(2):
                s = j - o
                value = tap(r, s).astype(BF16) if 0 <= s <= 2 else jnp.zeros((C, C), BF16)
                row = C * (4 * r + j)
                dst[row : row + C, C * o : C * o + C] = value


def write_weights_back(dst, tap):
    for r in range(3):
        for j in range(4):
            for o in range(2):
                s = j - o
                value = tap(2 - r, 2 - s).astype(BF16) if 0 <= s <= 2 else jnp.zeros((C, C), BF16)
                col = C * (4 * r + j)
                dst[C * o : C * o + C, col : col + C] = value


NN = (((1,), (0,)), ((), ()))
NT = (((1,), (1,)), ((), ()))
TN = (((0,), (0,)), ((), ()))


def dot(a, b, dims=NN):
    return lax.dot_general(a, b, dims, preferred_element_type=F32)


def rows_one(buf, i, q):
    return jnp.concatenate(
        [buf[i, r : r + 16, :, 256 * q : 256 * q + 512].reshape(256, 512) for r in range(3)], 1
    )


def rows_two(buf, first, number):
    return jnp.concatenate(
        [buf[pl.ds(first, number), r : r + 8].reshape(128 * number, 512) for r in range(3)], 1
    )


def by_two(count, work):
    def step(p, _):
        work(2 * p, 2)
        return 0

    loop(count // 2, step)

    @pl.when(count % 2 == 1)
    def _():
        work(count - 1, 1)


def conv_one(count, pairs, emit, dims=NN):
    def images(first, number):
        for n in range(number):
            for q in range(2):
                value = None
                for buf, weights in pairs:
                    term = dot(rows_one(buf, first + n, q), weights[...], dims)
                    value = term if value is None else value + term
                emit(first + n, q, value)

    by_two(count, images)


def conv_two(count, pairs, dst, dims=NN):
    def images(first, number):
        value = None
        for buf, weights in pairs:
            term = dot(rows_two(buf, 2 * first, 2 * number), weights[...], dims)
            value = term if value is None else value + term
        dst[pl.ds(2 * first, 2 * number)] = value.reshape(2 * number, 8, 16, 256)

    by_two((count + 1) // 2, images)


def kernel_grad_one(count, x, d, acc):
    acc[...] = jnp.zeros(acc.shape, F32)

    def images(first, number):
        places = [(first + n, q) for n in range(number) for q in range(2)]
        grads = jnp.concatenate(
            [d[i, 1:17, :, 128 + 256 * q : 384 + 256 * q].reshape(256, 256) for i, q in places], 0
        )
        for r in range(3):
            ins = jnp.concatenate(
                [x[i, r : r + 16, :, 256 * q : 256 * q + 512].reshape(256, 512) for i, q in places],
                0,
            )
            acc[r] += dot(ins, grads, TN)

    by_two(count, images)


def kernel_grad_two(count, pairs, acc):
    acc[...] = jnp.zeros(acc.shape, F32)

    def images(first, number):
        at, size = pl.ds(2 * first, 2 * number), 256 * number
        grads = jnp.concatenate([d[at, 1:9, :, 128:384].reshape(size, 256) for _, d in pairs], 0)
        for r in range(3):
            ins = jnp.concatenate([x[at, r : r + 8].reshape(size, 512) for x, _ in pairs], 0)
            acc[r] += dot(ins, grads, TN)

    by_two((count + 1) // 2, images)


def grad_tap(acc, r, s):
    return (
        acc[r, C * s : C * s + C, 0:C] + acc[r, C * (s + 1) : C * (s + 1) + C, C : 2 * C]
    )


def statistics(count, z, cells, tiles, chunk, blocks):
    steps = tiles // chunk

    def add(t, acc):
        i, start = t // steps, (t % steps) * chunk
        for m in range(blocks):
            acc = acc + total(get(z, i, start, chunk, m))
        return acc

    zero = jnp.zeros((8, C), F32)
    mean = channel(loop(count * steps, add, zero)) / cells

    def add_square(t, acc):
        i, start = t // steps, (t % steps) * chunk
        for m in range(blocks):
            centred = get(z, i, start, chunk, m) - mean
            acc = acc + total(centred * centred)
        return acc

    variance = channel(loop(count * steps, add_square, zero)) / cells
    return mean, lax.rsqrt(variance + EPSILON)


def activate(count, z, s1, s2, stats, gain, shift, tiles, chunk, blocks, emit):
    mean, inverse = stats
    steps = tiles // chunk

    def step(t, _):
        i, start = t // steps, (t % steps) * chunk
        for half in range(blocks // 2):
            pooled = None
            for m in (2 * half, 2 * half + 1):
                normed = (get(z, i, start, chunk, m) - mean) * inverse
                set_(z, i, start, chunk, m, normed)
                y = normed * gain + shift
                sig = 0.5 * jnp.tanh(0.5 * y) + 0.5
                a = y * sig
                rest = 1.0 - sig
                set_(s1, i, start, chunk, m, sig + a * rest)
                if s2 is not None:
                    set_(s2, i, start, chunk, m, sig * rest * (2.0 + y - 2.0 * a))
                part = jnp.sum(a, axis=1)
                pooled = part if pooled is None else pooled + part
            emit(i, start, half, pooled)
        return 0

    loop(count * steps, step)


def first_backward(count, zh, s1, up, dst, gain, inverse, cells, tiles, chunk, blocks):
    steps = tiles // chunk

    def add(t, carry):
        i, start = t // steps, (t % steps) * chunk
        one, two = carry
        for m in range(blocks):
            dy = up(i, start, m // 2) * get(s1, i, start, chunk, m)
            one = one + total(dy)
            two = two + total(dy * get(zh, i, start, chunk, m))
        return one, two

    zero = jnp.zeros((8, C), F32)
    one, two = loop(count * steps, add, (zero, zero))
    one, two = channel(one), channel(two)
    mean_one, mean_two = one / cells, two / cells
    scale = gain * inverse

    def step(t, _):
        i, start = t // steps, (t % steps) * chunk
        for m in range(blocks):
            dy = up(i, start, m // 2) * get(s1, i, start, chunk, m)
            dz = scale * (dy - mean_one - get(zh, i, start, chunk, m) * mean_two)
            put(dst, i, start, m, blocks, dz.reshape(-1, 8, C))
        return 0

    loop(count * steps, step)
    loop(count, lambda i, _: (put_halo(dst, i, tiles), 0)[1])
    return mean_one, mean_two, one, two


def clear_odd(count, buffers):
    @pl.when(count % 2 == 1)
    def _():
        for buf in buffers:
            buf[count] = jnp.zeros(buf.shape[1:], buf.dtype)


def mix_taps(weight, src, dst):
    for g in range(16):
        rows = slice(8 * g, 8 * g + 8)
        values = [src(f, rows) for f in range(9)]
        for q in range(9):
            acc = weight(q, 0) * values[0]
            for f in range(1, 9):
                acc = acc + weight(q, f) * values[f]
            dst(q, rows, acc)


def transform(acc, kernel, outer, inner, taps, g_low, t_one, t_two, fast):
    for f in range(9):
        g_low[:, C * f : C * f + C] = grad_tap(acc, f // 3, f % 3).astype(BF16)
    t_one[...] = dot(inner[...].astype(BF16), g_low[...])

    def write(q, rows, value):
        t_two[q, rows, :] = value

    mix_taps(
        lambda q, f: taps[q, f], lambda f, rows: t_one[rows, C * f : C * f + C], write
    )
    turned = dot(t_two[...].reshape(9 * C, C).astype(BF16), outer[...].astype(BF16), NT)
    fast[...] = kernel[...] - STEP_RATE * turned.reshape(9, C, C)


def transform_back(acc, outer, inner, taps, g_low, t_one, t_two, d_low, e, w, payload, u):
    for q in range(9):
        grad = grad_tap(acc, q // 3, q % 3)
        payload[C * q : C * q + C, :] = grad
        d_low[C * q : C * q + C, :] = (-STEP_RATE * grad).astype(BF16)
    e[...] = dot(d_low[...], outer[...].astype(BF16)).reshape(9, C, C)
    payload[AT_OUTER:AT_INNER, :] = dot(
        d_low[...], t_two[...].reshape(9 * C, C).astype(BF16), TN
    )

    def write(f, rows, value):
        w[rows, C * f : C * f + C] = value

    mix_taps(lambda f, q: taps[q, f], lambda q, rows: e[q, rows, :], write)
    w_low = w[...].astype(BF16)
    payload[AT_INNER:AT_SMALL, :] = dot(w_low, g_low[...], NT)
    u[...] = dot(inner[...].astype(BF16), w_low, TN)
    sums = []
    for q in range(9):
        for f in range(9):
            product = e[q] * t_one[:, C * f : C * f + C]
            sums.append(jnp.sum(product.reshape(16, 8, C), axis=0))
    sums = jnp.concatenate([jnp.sum(v, axis=0, keepdims=True) for v in sums], 0)
    sums = jnp.concatenate([jnp.sum(sums, axis=1, keepdims=True), jnp.zeros((7, 1), F32)], 0)
    spread = jnp.broadcast_to(sums, (88, C))
    row = lax.broadcasted_iota(jnp.int32, (88, C), 0)
    lane = lax.broadcasted_iota(jnp.int32, (88, C), 1)
    spread = jnp.where(row % 9 == lane, spread, 0.0)
    chosen = lax.broadcasted_iota(jnp.int32, (16, 88), 1) // 9 == lax.broadcasted_iota(
        jnp.int32, (16, 88), 0
    )
    payload[AT_SMALL : AT_SMALL + 16, :] = lax.dot_general(
        chosen.astype(F32), spread, NN, precision=lax.Precision.HIGHEST, preferred_element_type=F32
    )


def second_sums(count, c, zh, s1, up, cells, tiles, chunk, blocks):
    steps = tiles // chunk

    def add(t, carry):
        i, start = t // steps, (t % steps) * chunk
        one, two, three = carry
        for m in range(blocks):
            value = get(c, i, start, chunk, m)
            dy = up(i, start, m // 2) * get(s1, i, start, chunk, m)
            one = one + total(value)
            two = two + total(value * get(zh, i, start, chunk, m))
            three = three + total(value * dy)
        return one, two, three

    zero = jnp.zeros((8, C), F32)
    sums = loop(count * steps, add, (zero, zero, zero))
    return tuple(channel(v) / cells for v in sums)


def second_turn(count, c, zh, s1, s2, up, means, scale, emit, tiles, chunk, blocks):
    mean_c, mean_cz, _ = means
    steps = tiles // chunk

    def step(t, carry):
        i, start = t // steps, (t % steps) * chunk
        one, two = carry
        for half in range(blocks // 2):
            pooled = None
            for m in (2 * half, 2 * half + 1):
                normed = get(zh, i, start, chunk, m)
                cdy = scale * (get(c, i, start, chunk, m) - mean_c - normed * mean_cz)
                cy = cdy * up(i, start, half) * get(s2, i, start, chunk, m)
                set_(s2, i, start, chunk, m, cy)
                one = one + total(cy)
                two = two + total(cy * normed)
                if emit is not None:
                    part = jnp.sum(cdy * get(s1, i, start, chunk, m), axis=1)
                    pooled = part if pooled is None else pooled + part
            if emit is not None:
                emit(i, start, half, pooled)
        return one, two

    zero = jnp.zeros((8, C), F32)
    one, two = loop(count * steps, step, (zero, zero))
    return channel(one), channel(two)


def activation_sums(count, zh, s1, up, tiles, chunk, blocks):
    steps = tiles // chunk

    def add(t, carry):
        i, start = t // steps, (t % steps) * chunk
        one, two = carry
        for m in range(blocks):
            dy = up(i, start, m // 2) * get(s1, i, start, chunk, m)
            one = one + total(dy)
            two = two + total(dy * get(zh, i, start, chunk, m))
        return one, two

    zero = jnp.zeros((8, C), F32)
    one, two = loop(count * steps, add, (zero, zero))
    return channel(one), channel(two)


def second_close(
    count, c, zh, s1, t_buf, up, extra, dst, means, sums, first_means, gain, inverse, cells, tiles, chunk, blocks
):
    mean_c, mean_cz, mean_cdy = means
    mean_dy, mean_dyz = first_means
    mean_cy, mean_cyz = sums[0] / cells, sums[1] / cells
    scale = gain * inverse
    mean_cw = mean_cdy - mean_c * mean_dy - mean_cz * mean_dyz
    mean_z = gain * mean_cy - scale * (mean_c * mean_dyz + mean_dy * mean_cz)
    mean_zz = gain * mean_cyz - 2.0 * scale * mean_cz * mean_dyz
    alpha = inverse * gain
    beta = scale * inverse * mean_dyz
    gamma = scale * inverse * mean_cz
    delta = inverse * mean_z
    epsilon = inverse * (mean_zz + scale * mean_cw)
    steps = tiles // chunk

    def step(t, _):
        i, start = t // steps, (t % steps) * chunk
        for m in range(blocks):
            weight = -gamma * up(i, start, m // 2)
            if extra is not None:
                weight = weight + alpha * extra(i, start, m // 2)
            value = (
                alpha * get(t_buf, i, start, chunk, m)
                + weight * get(s1, i, start, chunk, m)
                - beta * get(c, i, start, chunk, m)
                - epsilon * get(zh, i, start, chunk, m)
                - delta
            )
            put(dst, i, start, m, blocks, value.reshape(-1, 8, C))
        return 0

    loop(count * steps, step)
    loop(count, lambda i, _: (put_halo(dst, i, tiles), 0)[1])
    return sums[1] + inverse * cells * mean_cw


def image_grads(count, pairs, dst, wide):
    def emit(i, q, value):
        for o in range(2):
            v = value[:, C * o : C * o + C].reshape(16, 2, 8, C)
            for b in range(2):
                wide[16 * b : 16 * b + 16, pl.ds(2 * q + o, 8, stride=4), :] = v[:, b]
        if q == 1:
            dst[i] = wide[...].astype(BF16)

    conv_one(count, pairs, emit, NT)

    def dead(i, _):
        dst[i] = jnp.zeros(dst.shape[1:], BF16)
        return 0

    lax.fori_loop(count, dst.shape[0], dead, 0)


def query_grad_kernel(count, grads, weights, after, dst, zeros, wide):
    zeros[0, 0] = 0.0
    image_grads(count[0], [(grads, weights)], dst, wide)


def support_grad_kernel(
    count, inner_grads, inner_weights, grads, kernel, after, dst, zeros, wide, weights
):
    zeros[0, 0] = 0.0
    write_weights_back(weights, lambda r, s: kernel[3 * r + s])
    image_grads(count[0], [(inner_grads, inner_weights), (grads, weights)], dst, wide)


def run_image_grads(kernel, name, shape, after, operands, scratch):
    vmem = pl.BlockSpec(memory_space=pltpu.VMEM)
    images = operands[1].shape[0]
    convs = (len(operands) - 1) // 2
    return pl.pallas_call(
        kernel,
        out_shape=(jax.ShapeDtypeStruct(shape, BF16), jax.ShapeDtypeStruct((1, 1), F32)),
        in_specs=[pl.BlockSpec(memory_space=pltpu.SMEM)]
        + [vmem] * (len(operands) - 1)
        + [pl.BlockSpec(memory_space=pl.ANY)],
        out_specs=(vmem, pl.BlockSpec(memory_space=pltpu.SMEM)),
        scratch_shapes=[pltpu.VMEM((32, 32, C), F32)] + scratch,
        compiler_params=pltpu.CompilerParams(vmem_limit_bytes=VMEM_SMALL),
        cost_estimate=pl.CostEstimate(
            flops=2 * images * convs * 1024 * 1536 * C,
            bytes_accessed=images * (convs + 1) * 32 * 32 * C * 2,
            transcendentals=0,
        ),
        name=name,
    )(*operands, after)


SCALARS = ["support_count", "query_count", "taps_one", "taps_two"]
NORMS = ["gain_one", "shift_one", "gain_two", "shift_two"]
AT_OUTER, AT_INNER, AT_SMALL, AT_GAIN, HALF_ROWS = 9 * C, 10 * C, 11 * C, 11 * C + 16, 11 * C + 32
QUARTER = HALF_ROWS // 4
FETCHED = [
    "kernel_one",
    "support",
    "kernel_two",
    "target",
    "inner_two",
    "outer_two",
    "inner_one",
    "outer_one",
    "query",
    "cotangent",
]
HELD = ["grad_q", "back_q", "grad_s", "back_s", "grad_e"]
KEPT = [f"keep_{at}" for at in range(4)]
SENT = HELD + KEPT + [f"send_{at}" for at in range(4)]


def scratch_of(s_cap, q_cap):
    def operand(count, tiles, blocks):
        return pltpu.VMEM((count, tiles + 2, 16, C * (blocks + 2)), BF16)

    def plain(count, tiles, blocks):
        return pltpu.VMEM((count, tiles, 16, C * blocks), F32)

    weights = pltpu.VMEM((1536, 256), BF16)
    weights_back = pltpu.VMEM((256, 1536), BF16)
    square = pltpu.VMEM((C, 9 * C), F32)
    square_low = pltpu.VMEM((C, 9 * C), BF16)
    stack = pltpu.VMEM((9, C, C), F32)
    s_even, q_even = s_cap + s_cap % 2, q_cap + q_cap % 2
    return dict(
        wide=pltpu.VMEM((32, 32, C), F32),
        xs=operand(s_cap, 16, 4),
        xq=operand(q_cap, 16, 4),
        ds=operand(s_cap, 16, 4),
        es=operand(s_cap, 16, 4),
        dq=operand(q_cap, 16, 4),
        zs=plain(s_cap, 16, 4),
        s1s=plain(s_cap, 16, 4),
        s2s=plain(s_cap, 16, 4),
        cs=plain(s_cap, 16, 4),
        zq=plain(q_cap, 16, 4),
        s1q=plain(q_cap, 16, 4),
        hs=operand(s_even, 8, 2),
        chs=operand(s_even, 8, 2),
        ds2=operand(s_even, 8, 2),
        es2=operand(s_even, 8, 2),
        hq=operand(q_even, 8, 2),
        dq2=operand(q_even, 8, 2),
        zs2=plain(s_even, 8, 2),
        s1s2=plain(s_even, 8, 2),
        s2s2=plain(s_even, 8, 2),
        cs2=plain(s_even, 8, 2),
        dhs=plain(s_even, 8, 2),
        chs_back=plain(s_even, 8, 2),
        zq2=plain(q_even, 8, 2),
        s1q2=plain(q_even, 8, 2),
        dhq=plain(q_even, 8, 2),
        w_a=weights,
        w_b=weights,
        w_c=weights,
        b_k2=weights_back,
        b_f1=weights_back,
        b_f2=weights_back,
        b_u1=weights_back,
        b_u2=weights_back,
        acc=pltpu.VMEM((3, 512, 256), F32),
        g_one=square_low,
        g_two=square_low,
        t1_one=square,
        t1_two=square,
        t2_one=stack,
        t2_two=stack,
        f_one=stack,
        f_two=stack,
        d_low=pltpu.VMEM((9 * C, C), BF16),
        e_buf=stack,
        w_buf=square,
        u_buf=square,
        payload=pltpu.VMEM((2, HALF_ROWS, C), F32),
        support_v=pltpu.VMEM((s_cap, 32, 32, C), BF16),
        query_v=pltpu.VMEM((q_cap, 32, 32, C), BF16),
        target_v=pltpu.VMEM((s_cap, 8, 8, C), BF16),
        cotangent_v=pltpu.VMEM((q_cap, 8, 8, C), BF16),
        kernel_one_v=stack,
        kernel_two_v=stack,
        inner_one_v=pltpu.VMEM((C, C), F32),
        outer_one_v=pltpu.VMEM((C, C), F32),
        inner_two_v=pltpu.VMEM((C, C), F32),
        outer_two_v=pltpu.VMEM((C, C), F32),
        fetch_sem=pltpu.SemaphoreType.DMA((len(FETCHED),)),
        send_sem=pltpu.SemaphoreType.DMA((len(SENT),)),
    )


def task_kernel(names, *refs):
    k = SimpleNamespace(**dict(zip(names, refs)))
    fetches = {}
    for n, name in enumerate(FETCHED):
        fetches[name] = pltpu.make_async_copy(getattr(k, name), getattr(k, name + "_v"), k.fetch_sem.at[n])
        fetches[name].start()
        setattr(k, name, getattr(k, name + "_v"))
    sent = []

    def ready(*wanted):
        for name in wanted:
            fetches[name].wait()

    def send(name, source, target=None):
        target = getattr(k, name) if target is None else target
        copy = pltpu.make_async_copy(source, target, k.send_sem.at[SENT.index(name)])
        copy.start()
        sent.append(copy)

    ns, nq = k.support_count[0], k.query_count[0]
    ns_f, nq_f = ns.astype(F32), nq.astype(F32)
    gain_one, shift_one, gain_two, shift_two = (
        jnp.broadcast_to(getattr(k, name)[...], (8, C)) for name in NORMS
    )
    pay_one, pay_two = k.payload.at[0], k.payload.at[1]
    one = dict(tiles=16, chunk=4, blocks=4)
    two = dict(tiles=8, chunk=8, blocks=2)
    wide = k.wide

    def load_images(count, src, dst):
        def image(i, _):
            wide[...] = src[i].astype(F32)
            for m in range(4):
                v = wide[:, pl.ds(m, 8, stride=4), :].reshape(2, 16, 1, 8, C)
                v = jnp.concatenate([v[0], v[1]], 1)
                put(dst, i, 0, m, 4, v.reshape(32, 8, C))
            put_halo(dst, i, 16)
            return 0

        loop(count, image)

    def keep(dst):
        def emit(i, q, value):
            dst[i, :, :, 256 * q : 256 * q + 256] = value.reshape(16, 16, 256)

        return emit

    def pool_to(dst):
        def emit(i, start, half, pooled):
            put(dst, i, start // 2, half, 2, (0.25 * pooled).reshape(-1, 8, C))

        return emit

    def finish(count, dst):
        loop(count, lambda i, _: (put_halo(dst, i, 8), 0)[1])

    def up_from(ref):
        def up(i, start, half):
            v = ref[i, pl.ds(start // 2, 2), :, C * half : C * half + C]
            return 0.25 * v.reshape(2, 1, 2, 8, C)

        return up

    def up_from_rows(ref, scale):
        def up(i, start, half):
            v = ref[i].astype(F32) * scale
            return jnp.concatenate([v[:4].reshape(4, 1, 1, 8, C), v[4:].reshape(4, 1, 1, 8, C)], 2)

        return up

    def tap_of(ref):
        return lambda r, s: ref[3 * r + s]

    def tap_wide(ref):
        return lambda r, s: ref[:, C * (3 * r + s) : C * (3 * r + s) + C]

    cells_one, cells_two = ns_f * 1024.0, ns_f * 256.0
    ready("kernel_one", "support")
    write_weights(k.w_a, tap_of(k.kernel_one))
    load_images(ns, k.support, k.xs)
    conv_one(ns, [(k.xs, k.w_a)], keep(k.zs))
    stats_one = statistics(ns, k.zs, cells_one, **one)
    activate(ns, k.zs, k.s1s, k.s2s, stats_one, gain_one, shift_one, emit=pool_to(k.hs), **one)
    finish(ns, k.hs)
    clear_odd(ns, [k.hs, k.chs, k.ds2, k.es2])
    ready("kernel_two", "target", "inner_two", "outer_two")
    write_weights(k.w_b, tap_of(k.kernel_two))
    conv_two(ns, [(k.hs, k.w_b)], k.zs2)
    stats_two = statistics(ns, k.zs2, cells_two, **two)
    activate(ns, k.zs2, k.s1s2, k.s2s2, stats_two, gain_two, shift_two, emit=lambda *a: None, **two)

    up_two = up_from_rows(k.target, 1.0 / (256.0 * ns_f))
    mean_dy2, mean_dyz2, _, _ = first_backward(
        ns, k.zs2, k.s1s2, up_two, k.ds2, gain_two, stats_two[1], cells_two, **two
    )
    kernel_grad_two(ns, [(k.hs, k.ds2)], k.acc)
    transform(
        k.acc, k.kernel_two, k.outer_two, k.inner_two, k.taps_two, k.g_two, k.t1_two, k.t2_two, k.f_two
    )
    write_weights_back(k.b_k2, tap_of(k.kernel_two))
    conv_two(ns, [(k.ds2, k.b_k2)], k.dhs, NT)
    up_one = up_from(k.dhs)
    mean_dy1, mean_dyz1, _, _ = first_backward(
        ns, k.zs, k.s1s, up_one, k.ds, gain_one, stats_one[1], cells_one, **one
    )
    send("grad_s", k.ds)
    ready("inner_one", "outer_one", "query", "cotangent")
    kernel_grad_one(ns, k.xs, k.ds, k.acc)
    transform(
        k.acc, k.kernel_one, k.outer_one, k.inner_one, k.taps_one, k.g_one, k.t1_one, k.t2_one, k.f_one
    )

    cells_q1, cells_q2 = nq_f * 1024.0, nq_f * 256.0
    write_weights(k.w_a, tap_of(k.f_one))
    load_images(nq, k.query, k.xq)
    conv_one(nq, [(k.xq, k.w_a)], keep(k.zq))
    stats_q1 = statistics(nq, k.zq, cells_q1, **one)
    activate(nq, k.zq, k.s1q, None, stats_q1, gain_one, shift_one, emit=pool_to(k.hq), **one)
    finish(nq, k.hq)
    clear_odd(nq, [k.hq, k.dq2])
    write_weights(k.w_c, tap_of(k.f_two))
    conv_two(nq, [(k.hq, k.w_c)], k.zq2)
    stats_q2 = statistics(nq, k.zq2, cells_q2, **two)

    def produce(i, start, half, pooled):
        v = 0.25 * pooled
        k.query_output[i] = jnp.concatenate([v[:, 0], v[:, 1]], 0).astype(BF16)

    activate(nq, k.zq2, k.s1q2, None, stats_q2, gain_two, shift_two, emit=produce, **two)

    def dead(i, _):
        k.query_output[i] = jnp.zeros(k.query_output.shape[1:], BF16)
        return 0

    lax.fori_loop(nq, k.query_output.shape[0], dead, 0)

    _, _, db2, dg2 = first_backward(
        nq, k.zq2, k.s1q2, up_from_rows(k.cotangent, 0.25 / nq_f), k.dq2, gain_two, stats_q2[1], cells_q2, **two
    )
    kernel_grad_two(nq, [(k.hq, k.dq2)], k.acc)
    transform_back(
        k.acc, k.outer_two, k.inner_two, k.taps_two, k.g_two, k.t1_two, k.t2_two, k.d_low, k.e_buf, k.w_buf,
        pay_two, k.u_buf,
    )
    write_weights_back(k.b_f2, tap_of(k.f_two))
    write_weights(k.w_c, tap_wide(k.u_buf))
    write_weights_back(k.b_u2, tap_wide(k.u_buf))
    conv_two(nq, [(k.dq2, k.b_f2)], k.dhq, NT)
    _, _, db1, dg1 = first_backward(
        nq, k.zq, k.s1q, up_from(k.dhq), k.dq, gain_one, stats_q1[1], cells_q1, **one
    )
    send("grad_q", k.dq)
    kernel_grad_one(nq, k.xq, k.dq, k.acc)
    transform_back(
        k.acc, k.outer_one, k.inner_one, k.taps_one, k.g_one, k.t1_one, k.t2_one, k.d_low, k.e_buf, k.w_buf,
        pay_one, k.u_buf,
    )
    write_weights_back(k.b_f1, tap_of(k.f_one))
    send("back_q", k.b_f1)
    write_weights(k.w_a, tap_wide(k.u_buf))
    write_weights_back(k.b_u1, tap_wide(k.u_buf))
    send("back_s", k.b_u1)

    conv_one(ns, [(k.xs, k.w_a)], keep(k.cs))
    means_one = second_sums(ns, k.cs, k.zs, k.s1s, up_one, cells_one, **one)
    turn_one = second_turn(
        ns, k.cs, k.zs, k.s1s, k.s2s, up_one, means_one, gain_one * stats_one[1], pool_to(k.chs), **one
    )
    finish(ns, k.chs)
    conv_two(ns, [(k.chs, k.w_b), (k.hs, k.w_c)], k.cs2)
    means_two = second_sums(ns, k.cs2, k.zs2, k.s1s2, up_two, cells_two, **two)
    turn_two = second_turn(
        ns, k.cs2, k.zs2, k.s1s2, k.s2s2, up_two, means_two, gain_two * stats_two[1], None, **two
    )
    extra_g2 = second_close(
        ns, k.cs2, k.zs2, k.s1s2, k.s2s2, up_two, None, k.es2, means_two, turn_two, (mean_dy2, mean_dyz2),
        gain_two, stats_two[1], cells_two, **two,
    )
    conv_two(ns, [(k.ds2, k.b_u2), (k.es2, k.b_k2)], k.chs_back, NT)
    kernel_grad_two(ns, [(k.chs, k.ds2), (k.hs, k.es2)], k.acc)
    for f in range(9):
        pay_two[C * f : C * f + C, :] += grad_tap(k.acc, f // 3, f % 3)
    up_back = up_from(k.chs_back)
    more = activation_sums(ns, k.zs, k.s1s, up_back, **one)
    turn_one = (turn_one[0] + more[0], turn_one[1] + more[1])
    extra_g1 = second_close(
        ns, k.cs, k.zs, k.s1s, k.s2s, up_one, up_back, k.es, means_one, turn_one, (mean_dy1, mean_dyz1),
        gain_one, stats_one[1], cells_one, **one,
    )
    send("grad_e", k.es)
    kernel_grad_one(ns, k.xs, k.es, k.acc)
    for f in range(9):
        pay_one[C * f : C * f + C, :] += grad_tap(k.acc, f // 3, f % 3)
    for pay, gain_grad, shift_grad in (
        (pay_one, dg1 + extra_g1, db1 + turn_one[0]),
        (pay_two, dg2 + extra_g2, db2 + turn_two[0]),
    ):
        pay[AT_GAIN : AT_GAIN + 2, :] = jnp.concatenate([gain_grad[0:1], shift_grad[0:1]], 0)
        pay[AT_GAIN + 2 :, :] = jnp.zeros((HALF_ROWS - AT_GAIN - 2, C), F32)
    half, place = my_place()
    for at in range(4):
        rows = pl.ds(pl.multiple_of((place ^ at) * QUARTER, 8), QUARTER)
        send(f"keep_{at}", k.payload.at[half, rows])
        send(f"send_{at}", k.payload.at[1 - half, rows], k.send.at[at])
    for copy in sent:
        copy.wait()


def run_task(values):
    s_cap, q_cap = values["support"].shape[0], values["query"].shape[0]
    scratch = scratch_of(s_cap, q_cap)
    vmem = pl.BlockSpec(memory_space=pltpu.VMEM)
    smem = pl.BlockSpec(memory_space=pltpu.SMEM)
    anywhere = pl.BlockSpec(memory_space=pl.ANY)

    def operand(count):
        return jax.ShapeDtypeStruct((count, 18, 16, 6 * C), BF16)

    back = jax.ShapeDtypeStruct((256, 1536), BF16)
    rows = jax.ShapeDtypeStruct((QUARTER, C), F32)
    inputs = SCALARS + NORMS + FETCHED
    outputs = ["query_output"] + HELD + KEPT + ["send"]
    results = pl.pallas_call(
        partial(task_kernel, inputs + outputs + list(scratch)),
        out_shape=(
            jax.ShapeDtypeStruct(values["cotangent"].shape, BF16),
            operand(q_cap),
            back,
            operand(s_cap),
            back,
            operand(s_cap),
            rows,
            rows,
            rows,
            rows,
            jax.ShapeDtypeStruct((4, QUARTER, C), F32),
        ),
        in_specs=[smem] * len(SCALARS) + [vmem] * len(NORMS) + [anywhere] * len(FETCHED),
        out_specs=[vmem] + [anywhere] * (len(outputs) - 1),
        scratch_shapes=list(scratch.values()),
        compiler_params=pltpu.CompilerParams(vmem_limit_bytes=VMEM_BYTES),
        name="task",
    )(*[values[name] for name in inputs])
    return dict(zip(outputs, results))


def swap(value, mask):
    extent = lax.axis_size(AXES)
    return lax.ppermute(value, AXES, [(place, place ^ mask) for place in range(extent)])


def sum_quarters(kept, sent, first, second):
    extent = lax.axis_size(AXES)
    come = swap(sent, 1)
    mine = {n: kept[n] + come[n] for n in (3, 1, 2, 0)}
    terms = {n: swap(mine[n], 2 * n) for n in (3, 1, 2)}
    one, zeros = first(come)
    part = mine[0] + terms[3] + terms[1] + terms[2] + zeros
    mask, two = 8, None
    while mask < extent:
        passed = swap(part, mask)
        if 2 * mask >= extent:
            two, zeros = second(part)
            passed = passed + zeros
        part = part + passed
        mask *= 2
    if two is None:
        two, _ = second(part)
    quarters = [part] + [swap(part, 2 * n) for n in (1, 2, 3)]
    return one, two, quarters, [swap(quarter, 1) for quarter in quarters]


def sum_plain(kept, sent, first, second):
    half, at = my_place()
    whole = jnp.stack([*kept, *sent]).reshape(2, 4, QUARTER, C)
    whole = jnp.where(half == 0, whole, whole[::-1])
    order = at ^ jnp.arange(4)
    whole = lax.psum(jnp.take(whole, order, axis=1), AXES)
    whole = jnp.take(jnp.where(half == 0, whole, whole[::-1]), order, axis=1)
    results = first(whole)[0], second(whole)[0]
    return *results, list(whole[0]), list(whole[1])


LAYER = ["outer", "inner", "taps"]


def my_place():
    me = lax.axis_index(AXES)
    return me & 1, (me >> 1) & 3


def finish_kernel(*refs):
    pieces, refs = refs[:8], refs[8:]
    factors, refs = refs[:6], refs[6:]
    results, refs = refs[:12], refs[12:]
    rest, rest_sem, kernel_sem = refs
    half, at = my_place()
    whole = AT_OUTER // QUARTER
    last = AT_OUTER - whole * QUARTER
    for n, piece in enumerate(pieces):
        quarter = at ^ (n % 4)
        for layer in range(2):
            kernel = results[6 * layer]
            own = half == layer if n < 4 else half != layer

            @pl.when(own & (quarter < whole))
            def _(piece=piece, kernel=kernel, quarter=quarter, layer=layer):
                start = pl.multiple_of(quarter * QUARTER, 8)
                pltpu.make_async_copy(
                    piece, kernel.at[pl.ds(start, QUARTER)], kernel_sem.at[layer]
                ).start()

            @pl.when(own & (quarter == whole))
            def _(piece=piece, kernel=kernel, layer=layer):
                pltpu.make_async_copy(
                    piece.at[pl.ds(last, QUARTER - last)], rest.at[layer], rest_sem.at[layer]
                ).start()
                pltpu.make_async_copy(
                    piece.at[pl.ds(0, last)], kernel.at[pl.ds(whole * QUARTER, last)], kernel_sem.at[layer]
                ).start()

    for layer in range(2):
        pltpu.make_async_copy(rest.at[layer], rest.at[layer], rest_sem.at[layer]).wait()
        kernel, gain, shift, outer, inner, taps = results[6 * layer : 6 * layer + 6]
        base = AT_GAIN - AT_OUTER
        gain[...] = rest[layer, base : base + 1, :]
        shift[...] = rest[layer, base + 1 : base + 2, :]
        for start, size, factor, result in zip(
            (0, C, 2 * C), (C, C, 9), factors[3 * layer : 3 * layer + 3], (outer, inner, taps)
        ):
            row = lax.broadcasted_iota(jnp.int32, (size, size), 0)
            column = lax.broadcasted_iota(jnp.int32, (size, size), 1)
            unit = jnp.where(row == column, 1.0, 0.0)
            value = rest[layer, start : start + size, :size]
            result[...] = value + 2.0 * PENALTY * (factor[...] - unit)
    for layer in range(2):
        kernel = results[6 * layer]
        pltpu.make_async_copy(kernel, kernel, kernel_sem.at[layer]).wait()


def run_finish(pieces, factors):
    vmem = pl.BlockSpec(memory_space=pltpu.VMEM)
    anywhere = pl.BlockSpec(memory_space=pl.ANY)

    def shape(*dims):
        return jax.ShapeDtypeStruct(dims, F32)

    layer = [shape(9 * C, C), shape(1, C), shape(1, C), shape(C, C), shape(C, C), shape(9, 9)]
    return pl.pallas_call(
        finish_kernel,
        out_shape=layer * 2,
        in_specs=[anywhere] * 8 + [vmem] * 6,
        out_specs=([anywhere] + [vmem] * 5) * 2,
        scratch_shapes=[
            pltpu.VMEM((2, HALF_ROWS - AT_OUTER, C), F32),
            pltpu.SemaphoreType.DMA((2,)),
            pltpu.SemaphoreType.DMA((2,)),
        ],
        compiler_params=pltpu.CompilerParams(vmem_limit_bytes=VMEM_SMALL),
        name="finish",
    )(*pieces, *factors)


def body(
    support_images,
    query_images,
    support_target,
    query_cotangent,
    support_count,
    query_count,
    kernel_one,
    kernel_two,
    gain_one,
    shift_one,
    gain_two,
    shift_two,
    outer_one,
    inner_one,
    taps_one,
    outer_two,
    inner_two,
    taps_two,
):
    shared = dict(
        taps_one=taps_one,
        taps_two=taps_two,
        kernel_one=kernel_one.reshape(9, C, C),
        kernel_two=kernel_two.reshape(9, C, C),
        gain_one=gain_one.reshape(1, C),
        shift_one=shift_one.reshape(1, C),
        gain_two=gain_two.reshape(1, C),
        shift_two=shift_two.reshape(1, C),
        outer_one=outer_one,
        inner_one=inner_one,
        outer_two=outer_two,
        inner_two=inner_two,
    )
    tasks = range(support_images.shape[0])
    results = [
        run_task(
            dict(
                shared,
                support_count=support_count[task : task + 1],
                query_count=query_count[task : task + 1],
                support=support_images[task],
                query=query_images[task],
                target=support_target[task],
                cotangent=query_cotangent[task],
            )
        )
        for task in tasks
    ]

    def query_grads(after):
        done = [
            run_image_grads(
                query_grad_kernel,
                "query_grad",
                query_images.shape[1:],
                after,
                [query_count[task : task + 1], results[task]["grad_q"], results[task]["back_q"]],
                [],
            )
            for task in tasks
        ]
        return jnp.stack([value for value, _ in done]), sum(zeros for _, zeros in done)

    def support_grads(after):
        done = [
            run_image_grads(
                support_grad_kernel,
                "support_grad",
                support_images.shape[1:],
                after,
                [
                    support_count[task : task + 1],
                    *[results[task][name] for name in ("grad_s", "back_s", "grad_e")],
                    shared["kernel_one"],
                ],
                [pltpu.VMEM((256, 1536), BF16)],
            )
            for task in tasks
        ]
        return jnp.stack([value for value, _ in done]), sum(zeros for _, zeros in done)

    kept = [sum(result[name] for result in results) for name in KEPT]
    sent = sum(result["send"] for result in results)
    extent = lax.axis_size(AXES)
    if extent < 8 or extent & (extent - 1):
        summed = sum_plain(kept, sent, query_grads, support_grads)
    else:
        summed = sum_quarters(kept, sent, query_grads, support_grads)
    query_grad, support_grad, mine, others = summed
    factors = [outer_one, inner_one, taps_one, outer_two, inner_two, taps_two]
    last = run_finish([*mine, *others], factors)
    return (
        jnp.stack([result["query_output"] for result in results]),
        support_grad,
        query_grad,
        last[0].reshape(3, 3, C, C),
        last[6].reshape(3, 3, C, C),
        *[last[at].reshape(C) for at in (1, 2, 7, 8)],
        *last[3:6],
        *last[9:12],
    )


def solution(mesh):
    split = P(("tasks", "group"))
    return jax.shard_map(
        body,
        mesh=mesh,
        in_specs=(split,) * 6 + (P(),) * 12,
        out_specs=(split,) * 3 + (P(),) * 12,
        check_vma=False,
    )
```

```python
from functools import partial
from types import SimpleNamespace

import jax
import jax.numpy as jnp
from jax import lax
from jax.experimental import pallas as pl
from jax.experimental.pallas import tpu as pltpu
from jax.sharding import PartitionSpec as P

STEP_RATE = 0.01
PENALTY = 1.0
EPSILON = 1e-05
C = 128
F32 = jnp.float32
BF16 = jnp.bfloat16
VMEM_BYTES = 57 << 20
VMEM_SMALL = 24 << 20
AXES = ("tasks", "group")


def shift_down(v):
    place = lax.broadcasted_iota(jnp.int32, v.shape, v.ndim - 2)
    return jnp.where(place == 0, 0.0, pltpu.roll(v, 1, v.ndim - 2))


def shift_up(v):
    place = lax.broadcasted_iota(jnp.int32, v.shape, v.ndim - 2)
    return jnp.where(place == 7, 0.0, pltpu.roll(v, 7, v.ndim - 2))


def put(buf, i, start, m, blocks, v):
    tiles = v.shape[0] // 2

    def store(block, value):
        buf[i, pl.ds(1 + start, tiles), :, C * block : C * block + C] = value.reshape(
            tiles, 16, C
        ).astype(BF16)

    store(1 + m, v)
    if m == 0:
        store(blocks + 1, shift_up(v))
    if m == blocks - 1:
        store(0, shift_down(v))


def put_halo(buf, i, tiles):
    last = buf[i, tiles].astype(F32)
    first = buf[i, 1].astype(F32)
    nothing = jnp.zeros((8, last.shape[1]), F32)
    buf[i, 0] = jnp.concatenate([nothing, last[:8]], 0).astype(BF16)
    buf[i, tiles + 1] = jnp.concatenate([first[8:], nothing], 0).astype(BF16)


def get(ref, i, start, tiles, m):
    return ref[i, pl.ds(start, tiles), :, C * m : C * m + C].reshape(tiles // 2, 2, 2, 8, C)


def set_(ref, i, start, tiles, m, v):
    ref[i, pl.ds(start, tiles), :, C * m : C * m + C] = v.reshape(tiles, 16, C)


def total(v):
    return jnp.sum(v.reshape(-1, 8, C), axis=0)


def channel(v):
    return jnp.broadcast_to(jnp.sum(v, axis=0, keepdims=True), (8, C))


def loop(count, body, carry=0):
    return lax.fori_loop(0, count, body, carry)


def write_weights(dst, tap):
    for r in range(3):
        for j in range(4):
            for o in range(2):
                s = j - o
                value = tap(r, s).astype(BF16) if 0 <= s <= 2 else jnp.zeros((C, C), BF16)
                row = C * (4 * r + j)
                dst[row : row + C, C * o : C * o + C] = value


def write_weights_back(dst, tap):
    for r in range(3):
        for j in range(4):
            for o in range(2):
                s = j - o
                value = tap(2 - r, 2 - s).astype(BF16) if 0 <= s <= 2 else jnp.zeros((C, C), BF16)
                col = C * (4 * r + j)
                dst[C * o : C * o + C, col : col + C] = value


NN = (((1,), (0,)), ((), ()))
NT = (((1,), (1,)), ((), ()))
TN = (((0,), (0,)), ((), ()))


def dot(a, b, dims=NN):
    return lax.dot_general(a, b, dims, preferred_element_type=F32)


def rows_one(buf, i, q):
    return jnp.concatenate(
        [buf[i, r : r + 16, :, 256 * q : 256 * q + 512].reshape(256, 512) for r in range(3)], 1
    )


def rows_two(buf, first, number):
    return jnp.concatenate(
        [buf[pl.ds(first, number), r : r + 8].reshape(128 * number, 512) for r in range(3)], 1
    )


def by_two(count, work):
    odd = count % 2 == 1

    @pl.when(odd)
    def _():
        work(count - 1, 1, True)

    @pl.when(jnp.logical_not(odd))
    def _():
        work(0, 2, True)

    def step(p, _):
        work(2 * p, 2, False)
        return 0

    lax.fori_loop(jnp.where(odd, 0, 1), count // 2, step, 0)


def conv_all(count, work):
    def step(p, _):
        work(2 * p, 2)
        return 0

    loop(count // 2, step)

    @pl.when(count % 2 == 1)
    def _():
        work(count - 1, 1)


def conv_one(count, pairs, emit, dims=NN):
    def images(first, number):
        for n in range(number):
            for q in range(2):
                value = None
                for buf, weights in pairs:
                    term = dot(rows_one(buf, first + n, q), weights[...], dims)
                    value = term if value is None else value + term
                emit(first + n, q, value)

    conv_all(count, images)


def conv_two(count, pairs, dst, dims=NN):
    def images(first, number):
        value = None
        for buf, weights in pairs:
            term = dot(rows_two(buf, 2 * first, 2 * number), weights[...], dims)
            value = term if value is None else value + term
        dst[pl.ds(2 * first, 2 * number)] = value.reshape(2 * number, 8, 16, 256)

    conv_all((count + 1) // 2, images)


def kernel_grad_one(count, x, d, acc):
    def images(first, number, fresh):
        places = [(first + n, q) for n in range(number) for q in range(2)]
        grads = jnp.concatenate(
            [d[i, 1:17, :, 128 + 256 * q : 384 + 256 * q].reshape(256, 256) for i, q in places], 0
        )
        for r in range(3):
            ins = jnp.concatenate(
                [x[i, r : r + 16, :, 256 * q : 256 * q + 512].reshape(256, 512) for i, q in places],
                0,
            )
            value = dot(ins, grads, TN)
            acc[r] = value if fresh else acc[r] + value

    by_two(count, images)


def kernel_grad_two(count, pairs, acc):
    def images(first, number, fresh):
        at, size = pl.ds(2 * first, 2 * number), 256 * number
        grads = jnp.concatenate([d[at, 1:9, :, 128:384].reshape(size, 256) for _, d in pairs], 0)
        for r in range(3):
            ins = jnp.concatenate([x[at, r : r + 8].reshape(size, 512) for x, _ in pairs], 0)
            value = dot(ins, grads, TN)
            acc[r] = value if fresh else acc[r] + value

    by_two((count + 1) // 2, images)


def grad_tap(acc, r, s):
    return (
        acc[r, C * s : C * s + C, 0:C] + acc[r, C * (s + 1) : C * (s + 1) + C, C : 2 * C]
    )


def statistics(count, z, cells, tiles, chunk, blocks, summed=None):
    steps = tiles // chunk

    def add(t, acc):
        i, start = t // steps, (t % steps) * chunk
        for m in range(blocks):
            acc = acc + total(get(z, i, start, chunk, m))
        return acc

    zero = jnp.zeros((8, C), F32)
    mean = channel(loop(count * steps, add, zero) if summed is None else summed) / cells

    def add_square(t, acc):
        i, start = t // steps, (t % steps) * chunk
        for m in range(blocks):
            centred = get(z, i, start, chunk, m) - mean
            acc = acc + total(centred * centred)
        return acc

    variance = channel(loop(count * steps, add_square, zero)) / cells
    return mean, lax.rsqrt(variance + EPSILON)


def activate(count, z, s1, s2, pools, stats, gain, shift, tiles, chunk, blocks, emit):
    mean, inverse = stats
    steps = tiles // chunk

    def step(t, _):
        i, start = t // steps, (t % steps) * chunk
        for half in range(blocks // 2):
            sums = []
            for m in (2 * half, 2 * half + 1):
                normed = (get(z, i, start, chunk, m) - mean) * inverse
                set_(z, i, start, chunk, m, normed)
                y = normed * gain + shift
                sig = 0.5 * jnp.tanh(0.5 * y) + 0.5
                a = y * sig
                rest = 1.0 - sig
                slope = sig + a * rest
                set_(s1, i, start, chunk, m, slope)
                if s2 is not None:
                    set_(s2, i, start, chunk, m, sig * rest * (2.0 + y - 2.0 * a))
                sums.append([jnp.sum(v, axis=1) for v in (a, slope, slope * normed)])
            pooled, *slopes = (one + two for one, two in zip(*sums))
            for ref, value in zip(pools, slopes):
                place = i, pl.ds(start // 2, chunk // 2), slice(None), slice(C * half, C * half + C)
                ref[place] = value.reshape(chunk // 2, 16, C)
            emit(i, start, half, pooled)
        return 0

    loop(count * steps, step)


def pooled_sums(count, pools, up, tiles, blocks):
    def add(i, carry):
        sums = list(carry)
        for half in range(blocks // 2):
            weight = up(i, 0, half).reshape(tiles // 2, 2, 8, C)
            for n, ref in enumerate(pools):
                value = ref[i, :, :, C * half : C * half + C].reshape(tiles // 2, 2, 8, C)
                sums[n] = sums[n] + total(weight * value)
        return tuple(sums)

    zero = jnp.zeros((8, C), F32)
    return tuple(channel(v) for v in loop(count, add, (zero, zero)))


def first_backward(count, zh, s1, pools, up, dst, gain, inverse, cells, tiles, chunk, blocks):
    steps = tiles // chunk
    one, two = pooled_sums(count, pools, up, tiles, blocks)
    mean_one, mean_two = one / cells, two / cells
    scale = gain * inverse

    def step(t, _):
        i, start = t // steps, (t % steps) * chunk
        for m in range(blocks):
            dy = up(i, start, m // 2) * get(s1, i, start, chunk, m)
            dz = scale * (dy - mean_one - get(zh, i, start, chunk, m) * mean_two)
            put(dst, i, start, m, blocks, dz.reshape(-1, 8, C))
        return 0

    loop(count * steps, step)
    loop(count, lambda i, _: (put_halo(dst, i, tiles), 0)[1])
    return mean_one, mean_two, one, two


def clear_odd(count, buffers):
    @pl.when(count % 2 == 1)
    def _():
        for buf in buffers:
            buf[count] = jnp.zeros(buf.shape[1:], buf.dtype)


def mix_taps(weight, src, dst):
    for g in range(16):
        rows = slice(8 * g, 8 * g + 8)
        values = [src(f, rows) for f in range(9)]
        for q in range(9):
            acc = weight(q, 0) * values[0]
            for f in range(1, 9):
                acc = acc + weight(q, f) * values[f]
            dst(q, rows, acc)


def transform(acc, kernel, outer, inner, taps, g_low, t_one, t_two, fast):
    for f in range(9):
        g_low[:, C * f : C * f + C] = grad_tap(acc, f // 3, f % 3).astype(BF16)
    t_one[...] = dot(inner[...].astype(BF16), g_low[...])

    def write(q, rows, value):
        t_two[q, rows, :] = value

    mix_taps(
        lambda q, f: taps[q, f], lambda f, rows: t_one[rows, C * f : C * f + C], write
    )
    turned = dot(t_two[...].reshape(9 * C, C).astype(BF16), outer[...].astype(BF16), NT)
    fast[...] = kernel[...] - STEP_RATE * turned.reshape(9, C, C)


def transform_back(acc, outer, inner, taps, g_low, t_one, t_two, d_low, e, w, payload, u):
    for q in range(9):
        grad = grad_tap(acc, q // 3, q % 3)
        payload[C * q : C * q + C, :] = grad
        d_low[C * q : C * q + C, :] = (-STEP_RATE * grad).astype(BF16)
    e[...] = dot(d_low[...], outer[...].astype(BF16)).reshape(9, C, C)
    payload[AT_OUTER:AT_INNER, :] = dot(
        d_low[...], t_two[...].reshape(9 * C, C).astype(BF16), TN
    )

    def write(f, rows, value):
        w[rows, C * f : C * f + C] = value

    mix_taps(lambda f, q: taps[q, f], lambda q, rows: e[q, rows, :], write)
    w_low = w[...].astype(BF16)
    payload[AT_INNER:AT_SMALL, :] = dot(w_low, g_low[...], NT)
    u[...] = dot(inner[...].astype(BF16), w_low, TN)
    sums = []
    for q in range(9):
        for f in range(9):
            product = e[q] * t_one[:, C * f : C * f + C]
            sums.append(jnp.sum(product.reshape(16, 8, C), axis=0))
    sums = jnp.concatenate([jnp.sum(v, axis=0, keepdims=True) for v in sums], 0)
    sums = jnp.concatenate([jnp.sum(sums, axis=1, keepdims=True), jnp.zeros((7, 1), F32)], 0)
    spread = jnp.broadcast_to(sums, (88, C))
    row = lax.broadcasted_iota(jnp.int32, (88, C), 0)
    lane = lax.broadcasted_iota(jnp.int32, (88, C), 1)
    spread = jnp.where(row % 9 == lane, spread, 0.0)
    chosen = lax.broadcasted_iota(jnp.int32, (16, 88), 1) // 9 == lax.broadcasted_iota(
        jnp.int32, (16, 88), 0
    )
    payload[AT_SMALL : AT_SMALL + 16, :] = lax.dot_general(
        chosen.astype(F32), spread, NN, precision=lax.Precision.HIGHEST, preferred_element_type=F32
    )


def second_sums(count, c, zh, s1, up, cells, tiles, chunk, blocks):
    steps = tiles // chunk

    def add(t, carry):
        i, start = t // steps, (t % steps) * chunk
        one, two, three = carry
        for m in range(blocks):
            value = get(c, i, start, chunk, m)
            dy = up(i, start, m // 2) * get(s1, i, start, chunk, m)
            one = one + total(value)
            two = two + total(value * get(zh, i, start, chunk, m))
            three = three + total(value * dy)
        return one, two, three

    zero = jnp.zeros((8, C), F32)
    sums = loop(count * steps, add, (zero, zero, zero))
    return tuple(channel(v) / cells for v in sums)


def second_turn(count, c, zh, s1, s2, up, means, scale, emit, tiles, chunk, blocks):
    mean_c, mean_cz, _ = means
    steps = tiles // chunk

    def step(t, carry):
        i, start = t // steps, (t % steps) * chunk
        one, two = carry
        for half in range(blocks // 2):
            pooled = None
            for m in (2 * half, 2 * half + 1):
                normed = get(zh, i, start, chunk, m)
                cdy = scale * (get(c, i, start, chunk, m) - mean_c - normed * mean_cz)
                cy = cdy * up(i, start, half) * get(s2, i, start, chunk, m)
                set_(s2, i, start, chunk, m, cy)
                one = one + total(cy)
                two = two + total(cy * normed)
                if emit is not None:
                    part = jnp.sum(cdy * get(s1, i, start, chunk, m), axis=1)
                    pooled = part if pooled is None else pooled + part
            if emit is not None:
                emit(i, start, half, pooled)
        return one, two

    zero = jnp.zeros((8, C), F32)
    one, two = loop(count * steps, step, (zero, zero))
    return channel(one), channel(two)


def second_close(
    count, c, zh, s1, t_buf, up, extra, dst, means, sums, first_means, gain, inverse, cells, tiles, chunk, blocks
):
    mean_c, mean_cz, mean_cdy = means
    mean_dy, mean_dyz = first_means
    mean_cy, mean_cyz = sums[0] / cells, sums[1] / cells
    scale = gain * inverse
    mean_cw = mean_cdy - mean_c * mean_dy - mean_cz * mean_dyz
    mean_z = gain * mean_cy - scale * (mean_c * mean_dyz + mean_dy * mean_cz)
    mean_zz = gain * mean_cyz - 2.0 * scale * mean_cz * mean_dyz
    alpha = inverse * gain
    beta = scale * inverse * mean_dyz
    gamma = scale * inverse * mean_cz
    delta = inverse * mean_z
    epsilon = inverse * (mean_zz + scale * mean_cw)
    steps = tiles // chunk

    def step(t, _):
        i, start = t // steps, (t % steps) * chunk
        for m in range(blocks):
            weight = -gamma * up(i, start, m // 2)
            if extra is not None:
                weight = weight + alpha * extra(i, start, m // 2)
            value = (
                alpha * get(t_buf, i, start, chunk, m)
                + weight * get(s1, i, start, chunk, m)
                - beta * get(c, i, start, chunk, m)
                - epsilon * get(zh, i, start, chunk, m)
                - delta
            )
            put(dst, i, start, m, blocks, value.reshape(-1, 8, C))
        return 0

    loop(count * steps, step)
    loop(count, lambda i, _: (put_halo(dst, i, tiles), 0)[1])
    return sums[1] + inverse * cells * mean_cw


def image_grads(count, pairs, dst, wide):
    def emit(i, q, value):
        for o in range(2):
            v = value[:, C * o : C * o + C].reshape(16, 2, 8, C)
            for b in range(2):
                wide[16 * b : 16 * b + 16, pl.ds(2 * q + o, 8, stride=4), :] = v[:, b]
        if q == 1:
            dst[i] = wide[...].astype(BF16)

    conv_one(count, pairs, emit, NT)

    def dead(i, _):
        dst[i] = jnp.zeros(dst.shape[1:], BF16)
        return 0

    lax.fori_loop(count, dst.shape[0], dead, 0)


def query_grad_kernel(count, grads, weights, after, dst, zeros, wide):
    zeros[...] = jnp.zeros(zeros.shape, F32)
    image_grads(count[0], [(grads, weights)], dst, wide)


def support_grad_kernel(
    count, inner_grads, inner_weights, grads, kernel, after, dst, zeros, wide, weights
):
    zeros[...] = jnp.zeros(zeros.shape, F32)
    write_weights_back(weights, lambda r, s: kernel[3 * r + s])
    image_grads(count[0], [(inner_grads, inner_weights), (grads, weights)], dst, wide)


def run_image_grads(kernel, name, shape, after, operands, scratch):
    vmem = pl.BlockSpec(memory_space=pltpu.VMEM)
    images = operands[1].shape[0]
    convs = (len(operands) - 1) // 2
    return pl.pallas_call(
        kernel,
        out_shape=(jax.ShapeDtypeStruct(shape, BF16), pltpu.VMEM((8, C), F32)),
        in_specs=[pl.BlockSpec(memory_space=pltpu.SMEM)]
        + [vmem] * (len(operands) - 1)
        + [pl.BlockSpec(memory_space=pl.ANY)],
        out_specs=(vmem, vmem),
        scratch_shapes=[pltpu.VMEM((32, 32, C), F32)] + scratch,
        compiler_params=pltpu.CompilerParams(vmem_limit_bytes=VMEM_SMALL),
        cost_estimate=pl.CostEstimate(
            flops=2 * images * convs * 1024 * 1536 * C,
            bytes_accessed=images * (convs + 1) * 32 * 32 * C * 2,
            transcendentals=0,
        ),
        name=name,
    )(*operands, after)


SCALARS = ["support_count", "query_count", "taps_one", "taps_two"]
NORMS = ["gain_one", "shift_one", "gain_two", "shift_two"]
AT_OUTER, AT_INNER, AT_SMALL, AT_GAIN, HALF_ROWS = 9 * C, 10 * C, 11 * C, 11 * C + 16, 11 * C + 32
QUARTER = HALF_ROWS // 4
FETCHED = [
    "kernel_one",
    "support",
    "kernel_two",
    "target",
    "inner_two",
    "outer_two",
    "inner_one",
    "outer_one",
    "query",
    "cotangent",
]
HELD = ["grad_q", "back_q", "grad_s", "back_s", "grad_e"]
KEPT = [f"keep_{at}" for at in range(4)]
GIVEN = [f"send_{at}" for at in range(4)]


def scratch_of(s_cap, q_cap):
    def operand(count, tiles, blocks):
        return pltpu.VMEM((count, tiles + 2, 16, C * (blocks + 2)), BF16)

    def plain(count, tiles, blocks):
        return pltpu.VMEM((count, tiles, 16, C * blocks), F32)

    weights = pltpu.VMEM((1536, 256), BF16)
    weights_back = pltpu.VMEM((256, 1536), BF16)
    square = pltpu.VMEM((C, 9 * C), F32)
    square_low = pltpu.VMEM((C, 9 * C), BF16)
    stack = pltpu.VMEM((9, C, C), F32)
    s_even, q_even = s_cap + s_cap % 2, q_cap + q_cap % 2
    return dict(
        wide=pltpu.VMEM((32, 32, C), F32),
        xs=operand(s_cap, 16, 4),
        xq=operand(q_cap, 16, 4),
        ds=operand(s_cap, 16, 4),
        dq=operand(q_cap, 16, 4),
        zs=plain(s_cap, 16, 4),
        s1s=plain(s_cap, 16, 4),
        s2s=plain(s_cap, 16, 4),
        zq=plain(q_cap, 16, 4),
        s1q=plain(q_cap, 16, 4),
        hs=operand(s_even, 8, 2),
        ds2=operand(s_even, 8, 2),
        hq=operand(q_even, 8, 2),
        dq2=operand(q_even, 8, 2),
        zs2=plain(s_even, 8, 2),
        s1s2=plain(s_even, 8, 2),
        s2s2=plain(s_even, 8, 2),
        dhs=plain(s_even, 8, 2),
        chs_back=plain(s_even, 8, 2),
        zq2=plain(q_even, 8, 2),
        s1q2=plain(q_even, 8, 2),
        dhq=plain(q_even, 8, 2),
        p1s=plain(s_cap, 8, 2),
        p2s=plain(s_cap, 8, 2),
        p1s2=plain(s_cap, 4, 1),
        p2s2=plain(s_cap, 4, 1),
        p1q=plain(q_cap, 8, 2),
        p2q=plain(q_cap, 8, 2),
        p1q2=plain(q_cap, 4, 1),
        p2q2=plain(q_cap, 4, 1),
        sums=pltpu.VMEM((3, 8, C), F32),
        w_a=weights,
        w_b=weights,
        w_c=weights,
        b_k2=weights_back,
        b_f1=weights_back,
        b_f2=weights_back,
        b_u1=weights_back,
        b_u2=weights_back,
        acc=pltpu.VMEM((3, 512, 256), F32),
        g_one=square_low,
        g_two=square_low,
        t1_one=square,
        t1_two=square,
        t2_one=stack,
        t2_two=stack,
        f_one=stack,
        f_two=stack,
        d_low=pltpu.VMEM((9 * C, C), BF16),
        e_buf=stack,
        w_buf=square,
        u_buf=square,
        payload=pltpu.VMEM((2, HALF_ROWS, C), F32),
        support_v=pltpu.VMEM((s_cap, 32, 32, C), BF16),
        query_v=pltpu.VMEM((q_cap, 32, 32, C), BF16),
        target_v=pltpu.VMEM((s_cap, 8, 8, C), BF16),
        cotangent_v=pltpu.VMEM((q_cap, 8, 8, C), BF16),
        kernel_one_v=stack,
        kernel_two_v=stack,
        inner_one_v=pltpu.VMEM((C, C), F32),
        outer_one_v=pltpu.VMEM((C, C), F32),
        inner_two_v=pltpu.VMEM((C, C), F32),
        outer_two_v=pltpu.VMEM((C, C), F32),
        fetch_sem=pltpu.SemaphoreType.DMA((len(FETCHED),)),
        send_sem=pltpu.SemaphoreType.DMA((len(HELD),)),
    )


def task_kernel(names, *refs):
    k = SimpleNamespace(**dict(zip(names, refs)))
    fetches = {}
    for n, name in enumerate(FETCHED):
        fetches[name] = pltpu.make_async_copy(getattr(k, name), getattr(k, name + "_v"), k.fetch_sem.at[n])
        setattr(k, name, getattr(k, name + "_v"))
    for name in FETCHED[:2]:
        fetches[name].start()
    sent = []

    def ready(*wanted):
        for name in wanted:
            fetches[name].wait()

    def send(name, source):
        copy = pltpu.make_async_copy(source, getattr(k, name), k.send_sem.at[HELD.index(name)])
        copy.start()
        sent.append(copy)

    def close_layer(layer, gain_grad, shift_grad):
        pay = k.payload.at[layer]
        pay[AT_GAIN : AT_GAIN + 2, :] = jnp.concatenate([gain_grad[0:1], shift_grad[0:1]], 0)
        pay[AT_GAIN + 2 :, :] = jnp.zeros((HALF_ROWS - AT_GAIN - 2, C), F32)
        half, place = my_place()
        for at in range(4):
            rows = pl.ds(pl.multiple_of((place ^ at) * QUARTER, 8), QUARTER)
            for kept in (True, False):
                target = getattr(k, f"keep_{at}" if kept else f"send_{at}")

                @pl.when(half == (layer if kept else 1 - layer))
                def _(target=target, rows=rows):
                    target[...] = pay[rows, :]

    ns, nq = k.support_count[0], k.query_count[0]
    ns_f, nq_f = ns.astype(F32), nq.astype(F32)
    gain_one, shift_one, gain_two, shift_two = (
        jnp.broadcast_to(getattr(k, name)[...], (8, C)) for name in NORMS
    )
    pay_one, pay_two = k.payload.at[0], k.payload.at[1]
    k.cs, k.es, k.cs2, k.es2, k.chs = k.zq, k.xq, k.zq2, k.hq, k.dq2
    one = dict(tiles=16, chunk=16, blocks=4)
    two = dict(tiles=8, chunk=8, blocks=2)
    wide = k.wide

    def load_images(count, src, dst):
        def image(i, _):
            wide[...] = src[i].astype(F32)
            for m in range(4):
                v = wide[:, pl.ds(m, 8, stride=4), :].reshape(2, 16, 1, 8, C)
                v = jnp.concatenate([v[0], v[1]], 1)
                put(dst, i, 0, m, 4, v.reshape(32, 8, C))
            put_halo(dst, i, 16)
            return 0

        loop(count, image)

    def keep(dst, terms):
        k.sums[...] = jnp.zeros(k.sums.shape, F32)

        def emit(i, q, value):
            dst[i, :, :, 256 * q : 256 * q + 256] = value.reshape(16, 16, 256)
            added = None
            for o in range(2):
                block = value[:, C * o : C * o + C].reshape(8, 2, 2, 8, C)
                parts = [total(term) for term in terms(i, 2 * q + o, block)]
                added = parts if added is None else [v + w for v, w in zip(added, parts)]
            for n, part in enumerate(added):
                k.sums[n] += part

        return emit

    def alone(i, m, block):
        return [block]

    def pool_to(dst):
        def emit(i, start, half, pooled):
            put(dst, i, start // 2, half, 2, (0.25 * pooled).reshape(-1, 8, C))

        return emit

    def finish(count, dst):
        loop(count, lambda i, _: (put_halo(dst, i, 8), 0)[1])

    def up_from(ref):
        def up(i, start, half):
            number = one["chunk"] // 2
            v = ref[i, pl.ds(start // 2, number), :, C * half : C * half + C]
            return 0.25 * v.reshape(number, 1, 2, 8, C)

        return up

    def up_from_rows(ref, scale):
        def up(i, start, half):
            v = ref[i].astype(F32) * scale
            return jnp.concatenate([v[:4].reshape(4, 1, 1, 8, C), v[4:].reshape(4, 1, 1, 8, C)], 2)

        return up

    def tap_of(ref):
        return lambda r, s: ref[3 * r + s]

    def tap_wide(ref):
        return lambda r, s: ref[:, C * (3 * r + s) : C * (3 * r + s) + C]

    pools_one, pools_two = (k.p1s, k.p2s), (k.p1s2, k.p2s2)
    pools_q1, pools_q2 = (k.p1q, k.p2q), (k.p1q2, k.p2q2)

    cells_one, cells_two = ns_f * 1024.0, ns_f * 256.0
    ready("kernel_one")
    write_weights(k.w_a, tap_of(k.kernel_one))
    ready("support")
    for name in FETCHED[2:]:
        fetches[name].start()
    load_images(ns, k.support, k.xs)
    conv_one(ns, [(k.xs, k.w_a)], keep(k.zs, alone))
    stats_one = statistics(ns, k.zs, cells_one, summed=k.sums[0], **one)
    activate(ns, k.zs, k.s1s, k.s2s, pools_one, stats_one, gain_one, shift_one, emit=pool_to(k.hs), **one)
    finish(ns, k.hs)
    clear_odd(ns, [k.hs, k.ds2])
    ready("kernel_two", "target", "inner_two", "outer_two")
    write_weights(k.w_b, tap_of(k.kernel_two))
    conv_two(ns, [(k.hs, k.w_b)], k.zs2)
    stats_two = statistics(ns, k.zs2, cells_two, **two)
    activate(ns, k.zs2, k.s1s2, k.s2s2, pools_two, stats_two, gain_two, shift_two, emit=lambda *a: None, **two)

    up_two = up_from_rows(k.target, 1.0 / (256.0 * ns_f))
    mean_dy2, mean_dyz2, _, _ = first_backward(
        ns, k.zs2, k.s1s2, pools_two, up_two, k.ds2, gain_two, stats_two[1], cells_two, **two
    )
    kernel_grad_two(ns, [(k.hs, k.ds2)], k.acc)
    transform(
        k.acc, k.kernel_two, k.outer_two, k.inner_two, k.taps_two, k.g_two, k.t1_two, k.t2_two, k.f_two
    )
    write_weights_back(k.b_k2, tap_of(k.kernel_two))
    conv_two(ns, [(k.ds2, k.b_k2)], k.dhs, NT)
    up_one = up_from(k.dhs)
    mean_dy1, mean_dyz1, _, _ = first_backward(
        ns, k.zs, k.s1s, pools_one, up_one, k.ds, gain_one, stats_one[1], cells_one, **one
    )
    send("grad_s", k.ds)
    ready("inner_one", "outer_one", "query", "cotangent")
    kernel_grad_one(ns, k.xs, k.ds, k.acc)
    transform(
        k.acc, k.kernel_one, k.outer_one, k.inner_one, k.taps_one, k.g_one, k.t1_one, k.t2_one, k.f_one
    )

    cells_q1, cells_q2 = nq_f * 1024.0, nq_f * 256.0
    write_weights(k.w_a, tap_of(k.f_one))
    load_images(nq, k.query, k.xq)
    conv_one(nq, [(k.xq, k.w_a)], keep(k.zq, alone))
    stats_q1 = statistics(nq, k.zq, cells_q1, summed=k.sums[0], **one)
    activate(nq, k.zq, k.s1q, None, pools_q1, stats_q1, gain_one, shift_one, emit=pool_to(k.hq), **one)
    finish(nq, k.hq)
    clear_odd(nq, [k.hq, k.dq2])
    write_weights(k.w_c, tap_of(k.f_two))
    conv_two(nq, [(k.hq, k.w_c)], k.zq2)
    stats_q2 = statistics(nq, k.zq2, cells_q2, **two)

    def produce(i, start, half, pooled):
        v = 0.25 * pooled
        k.query_output[i] = jnp.concatenate([v[:, 0], v[:, 1]], 0).astype(BF16)

    activate(nq, k.zq2, k.s1q2, None, pools_q2, stats_q2, gain_two, shift_two, emit=produce, **two)

    def dead(i, _):
        k.query_output[i] = jnp.zeros(k.query_output.shape[1:], BF16)
        return 0

    lax.fori_loop(nq, k.query_output.shape[0], dead, 0)

    _, _, db2, dg2 = first_backward(
        nq, k.zq2, k.s1q2, pools_q2, up_from_rows(k.cotangent, 0.25 / nq_f), k.dq2, gain_two, stats_q2[1], cells_q2, **two
    )
    kernel_grad_two(nq, [(k.hq, k.dq2)], k.acc)
    transform_back(
        k.acc, k.outer_two, k.inner_two, k.taps_two, k.g_two, k.t1_two, k.t2_two, k.d_low, k.e_buf, k.w_buf,
        pay_two, k.u_buf,
    )
    write_weights_back(k.b_f2, tap_of(k.f_two))
    write_weights(k.w_c, tap_wide(k.u_buf))
    write_weights_back(k.b_u2, tap_wide(k.u_buf))
    conv_two(nq, [(k.dq2, k.b_f2)], k.dhq, NT)
    _, _, db1, dg1 = first_backward(
        nq, k.zq, k.s1q, pools_q1, up_from(k.dhq), k.dq, gain_one, stats_q1[1], cells_q1, **one
    )
    send("grad_q", k.dq)
    kernel_grad_one(nq, k.xq, k.dq, k.acc)
    transform_back(
        k.acc, k.outer_one, k.inner_one, k.taps_one, k.g_one, k.t1_one, k.t2_one, k.d_low, k.e_buf, k.w_buf,
        pay_one, k.u_buf,
    )
    write_weights_back(k.b_f1, tap_of(k.f_one))
    send("back_q", k.b_f1)
    write_weights(k.w_a, tap_wide(k.u_buf))
    write_weights_back(k.b_u1, tap_wide(k.u_buf))
    send("back_s", k.b_u1)

    clear_odd(ns, [k.chs, k.es2])

    def second_terms(i, m, block):
        dy = up_one(i, 0, m // 2) * get(k.s1s, i, 0, 16, m)
        return [block, block * get(k.zs, i, 0, 16, m), block * dy]

    conv_one(ns, [(k.xs, k.w_a)], keep(k.cs, second_terms))
    means_one = tuple(channel(k.sums[n]) / cells_one for n in range(3))
    turn_one = second_turn(
        ns, k.cs, k.zs, k.s1s, k.s2s, up_one, means_one, gain_one * stats_one[1], pool_to(k.chs), **one
    )
    finish(ns, k.chs)
    conv_two(ns, [(k.chs, k.w_b), (k.hs, k.w_c)], k.cs2)
    means_two = second_sums(ns, k.cs2, k.zs2, k.s1s2, up_two, cells_two, **two)
    turn_two = second_turn(
        ns, k.cs2, k.zs2, k.s1s2, k.s2s2, up_two, means_two, gain_two * stats_two[1], None, **two
    )
    extra_g2 = second_close(
        ns, k.cs2, k.zs2, k.s1s2, k.s2s2, up_two, None, k.es2, means_two, turn_two, (mean_dy2, mean_dyz2),
        gain_two, stats_two[1], cells_two, **two,
    )
    conv_two(ns, [(k.ds2, k.b_u2), (k.es2, k.b_k2)], k.chs_back, NT)
    kernel_grad_two(ns, [(k.chs, k.ds2), (k.hs, k.es2)], k.acc)
    for f in range(9):
        pay_two[C * f : C * f + C, :] += grad_tap(k.acc, f // 3, f % 3)
    close_layer(1, dg2 + extra_g2, db2 + turn_two[0])
    up_back = up_from(k.chs_back)
    more = pooled_sums(ns, pools_one, up_back, 16, 4)
    turn_one = (turn_one[0] + more[0], turn_one[1] + more[1])
    extra_g1 = second_close(
        ns, k.cs, k.zs, k.s1s, k.s2s, up_one, up_back, k.es, means_one, turn_one, (mean_dy1, mean_dyz1),
        gain_one, stats_one[1], cells_one, **one,
    )
    send("grad_e", k.es.at[pl.ds(0, k.xs.shape[0])])
    kernel_grad_one(ns, k.xs, k.es, k.acc)
    for f in range(9):
        pay_one[C * f : C * f + C, :] += grad_tap(k.acc, f // 3, f % 3)
    close_layer(0, dg1 + extra_g1, db1 + turn_one[0])
    for copy in sent:
        copy.wait()


def run_task(values):
    s_cap, q_cap = values["support"].shape[0], values["query"].shape[0]
    scratch = scratch_of(s_cap, q_cap)
    vmem = pl.BlockSpec(memory_space=pltpu.VMEM)
    smem = pl.BlockSpec(memory_space=pltpu.SMEM)
    anywhere = pl.BlockSpec(memory_space=pl.ANY)

    def operand(count):
        return jax.ShapeDtypeStruct((count, 18, 16, 6 * C), BF16)

    back = jax.ShapeDtypeStruct((256, 1536), BF16)
    rows = pltpu.VMEM((QUARTER, C), F32)
    inputs = SCALARS + NORMS + FETCHED
    outputs = ["query_output"] + HELD + KEPT + GIVEN
    results = pl.pallas_call(
        partial(task_kernel, inputs + outputs + list(scratch)),
        out_shape=(
            jax.ShapeDtypeStruct(values["cotangent"].shape, BF16),
            operand(q_cap),
            back,
            operand(s_cap),
            back,
            operand(s_cap),
            *[rows] * 8,
        ),
        in_specs=[smem] * len(SCALARS) + [vmem] * len(NORMS) + [anywhere] * len(FETCHED),
        out_specs=[vmem] + [anywhere] * len(HELD) + [vmem] * 8,
        scratch_shapes=list(scratch.values()),
        compiler_params=pltpu.CompilerParams(vmem_limit_bytes=VMEM_BYTES),
        name="task",
    )(*[values[name] for name in inputs])
    return dict(zip(outputs, results))


def swap(value, mask):
    extent = lax.axis_size(AXES)
    return lax.ppermute(value, AXES, [(place, place ^ mask) for place in range(extent)])


def sum_quarters(kept, sent, first, second):
    extent = lax.axis_size(AXES)
    come = {n: swap(sent[n], 1) for n in (3, 1, 2, 0)}
    mine = {n: kept[n] + come[n] for n in (3, 1, 2, 0)}
    terms = {n: swap(mine[n], 2 * n) for n in (3, 1, 2)}
    one, zeros = first(come[0][0:8])
    part = mine[0] + terms[3] + terms[1] + terms[2] + zeros[0:1]
    mask, two = 8, None
    while mask < extent:
        passed = swap(part, mask)
        if 2 * mask >= extent:
            two, zeros = second(part[0:8])
            passed = passed + zeros[0:1]
        part = part + passed
        mask *= 2
    if two is None:
        two, _ = second(part[0:8])
    quarters = [part] + [swap(part, 2 * n) for n in (1, 2, 3)]
    return one, two, quarters, [swap(quarter, 1) for quarter in quarters]


def sum_plain(kept, sent, first, second):
    half, at = my_place()
    whole = jnp.stack([*kept, *sent]).reshape(2, 4, QUARTER, C)
    whole = jnp.where(half == 0, whole, whole[::-1])
    order = at ^ jnp.arange(4)
    whole = lax.psum(jnp.take(whole, order, axis=1), AXES)
    whole = jnp.take(jnp.where(half == 0, whole, whole[::-1]), order, axis=1)
    results = first(whole)[0], second(whole)[0]
    return *results, list(whole[0]), list(whole[1])


LAYER = ["outer", "inner", "taps"]


def my_place():
    me = lax.axis_index(AXES)
    return me & 1, (me >> 1) & 3


def finish_kernel(*refs):
    pieces, refs = refs[:8], refs[8:]
    factors, refs = refs[:6], refs[6:]
    results, refs = refs[:12], refs[12:]
    rest, kernel_sem = refs
    half, at = my_place()
    whole = AT_OUTER // QUARTER
    last = AT_OUTER - whole * QUARTER
    for n, piece in enumerate(pieces):
        quarter = at ^ (n % 4)
        for layer in range(2):
            kernel = results[6 * layer]
            own = half == layer if n < 4 else half != layer

            @pl.when(own & (quarter < whole))
            def _(piece=piece, kernel=kernel, quarter=quarter, layer=layer):
                start = pl.multiple_of(quarter * QUARTER, 8)
                pltpu.make_async_copy(
                    piece, kernel.at[pl.ds(start, QUARTER)], kernel_sem.at[layer]
                ).start()

            @pl.when(own & (quarter == whole))
            def _(piece=piece, kernel=kernel, layer=layer):
                rest[layer] = piece[last:QUARTER, :]
                pltpu.make_async_copy(
                    piece.at[pl.ds(0, last)], kernel.at[pl.ds(whole * QUARTER, last)], kernel_sem.at[layer]
                ).start()

    for layer in range(2):
        kernel, gain, shift, outer, inner, taps = results[6 * layer : 6 * layer + 6]
        base = AT_GAIN - AT_OUTER
        gain[...] = rest[layer, base : base + 1, :]
        shift[...] = rest[layer, base + 1 : base + 2, :]
        for start, size, factor, result in zip(
            (0, C, 2 * C), (C, C, 9), factors[3 * layer : 3 * layer + 3], (outer, inner, taps)
        ):
            row = lax.broadcasted_iota(jnp.int32, (size, size), 0)
            column = lax.broadcasted_iota(jnp.int32, (size, size), 1)
            unit = jnp.where(row == column, 1.0, 0.0)
            value = rest[layer, start : start + size, :size]
            result[...] = value + 2.0 * PENALTY * (factor[...] - unit)
    for layer in range(2):
        kernel = results[6 * layer]
        pltpu.make_async_copy(kernel, kernel, kernel_sem.at[layer]).wait()


def run_finish(pieces, factors):
    vmem = pl.BlockSpec(memory_space=pltpu.VMEM)
    anywhere = pl.BlockSpec(memory_space=pl.ANY)

    def shape(*dims):
        return jax.ShapeDtypeStruct(dims, F32)

    layer = [shape(9 * C, C), shape(1, C), shape(1, C), shape(C, C), shape(C, C), shape(9, 9)]
    return pl.pallas_call(
        finish_kernel,
        out_shape=layer * 2,
        in_specs=[vmem] * 14,
        out_specs=([anywhere] + [vmem] * 5) * 2,
        scratch_shapes=[
            pltpu.VMEM((2, HALF_ROWS - AT_OUTER, C), F32),
            pltpu.SemaphoreType.DMA((2,)),
        ],
        compiler_params=pltpu.CompilerParams(vmem_limit_bytes=VMEM_SMALL),
        name="finish",
    )(*pieces, *factors)


def body(
    support_images,
    query_images,
    support_target,
    query_cotangent,
    support_count,
    query_count,
    kernel_one,
    kernel_two,
    gain_one,
    shift_one,
    gain_two,
    shift_two,
    outer_one,
    inner_one,
    taps_one,
    outer_two,
    inner_two,
    taps_two,
):
    shared = dict(
        taps_one=taps_one,
        taps_two=taps_two,
        kernel_one=kernel_one.reshape(9, C, C),
        kernel_two=kernel_two.reshape(9, C, C),
        gain_one=gain_one.reshape(1, C),
        shift_one=shift_one.reshape(1, C),
        gain_two=gain_two.reshape(1, C),
        shift_two=shift_two.reshape(1, C),
        outer_one=outer_one,
        inner_one=inner_one,
        outer_two=outer_two,
        inner_two=inner_two,
    )
    tasks = range(support_images.shape[0])
    results = [
        run_task(
            dict(
                shared,
                support_count=support_count[task : task + 1],
                query_count=query_count[task : task + 1],
                support=support_images[task],
                query=query_images[task],
                target=support_target[task],
                cotangent=query_cotangent[task],
            )
        )
        for task in tasks
    ]

    def query_grads(after):
        done = [
            run_image_grads(
                query_grad_kernel,
                "query_grad",
                query_images.shape[1:],
                after,
                [query_count[task : task + 1], results[task]["grad_q"], results[task]["back_q"]],
                [],
            )
            for task in tasks
        ]
        return jnp.stack([value for value, _ in done]), sum(zeros for _, zeros in done)

    def support_grads(after):
        done = [
            run_image_grads(
                support_grad_kernel,
                "support_grad",
                support_images.shape[1:],
                after,
                [
                    support_count[task : task + 1],
                    *[results[task][name] for name in ("grad_s", "back_s", "grad_e")],
                    shared["kernel_one"],
                ],
                [pltpu.VMEM((256, 1536), BF16)],
            )
            for task in tasks
        ]
        return jnp.stack([value for value, _ in done]), sum(zeros for _, zeros in done)

    kept = [sum(result[name] for result in results) for name in KEPT]
    sent = [sum(result[name] for result in results) for name in GIVEN]
    extent = lax.axis_size(AXES)
    if extent < 8 or extent & (extent - 1):
        summed = sum_plain(kept, sent, query_grads, support_grads)
    else:
        summed = sum_quarters(kept, sent, query_grads, support_grads)
    query_grad, support_grad, mine, others = summed
    factors = [outer_one, inner_one, taps_one, outer_two, inner_two, taps_two]
    last = run_finish([*mine, *others], factors)
    return (
        jnp.stack([result["query_output"] for result in results]),
        support_grad,
        query_grad,
        last[0].reshape(3, 3, C, C),
        last[6].reshape(3, 3, C, C),
        *[last[at].reshape(C) for at in (1, 2, 7, 8)],
        *last[3:6],
        *last[9:12],
    )


def solution(mesh):
    split = P(("tasks", "group"))
    return jax.shard_map(
        body,
        mesh=mesh,
        in_specs=(split,) * 6 + (P(),) * 12,
        out_specs=(split,) * 3 + (P(),) * 12,
        check_vma=False,
    )
```

```python
from functools import partial
from types import SimpleNamespace

import jax
import jax.numpy as jnp
from jax import lax
from jax.experimental import pallas as pl
from jax.experimental.pallas import tpu as pltpu
from jax.sharding import PartitionSpec as P

STEP_RATE = 0.01
PENALTY = 1.0
EPSILON = 1e-05
C = 128
F32 = jnp.float32
BF16 = jnp.bfloat16
VMEM_BYTES = 57 << 20
VMEM_SMALL = 24 << 20
MIX_ROWS = 64
AXES = ("tasks", "group")


def shift_down(v):
    place = lax.broadcasted_iota(jnp.int32, v.shape, v.ndim - 2)
    return jnp.where(place == 0, 0.0, pltpu.roll(v, 1, v.ndim - 2))


def shift_up(v):
    place = lax.broadcasted_iota(jnp.int32, v.shape, v.ndim - 2)
    return jnp.where(place == 7, 0.0, pltpu.roll(v, 7, v.ndim - 2))


def put(buf, i, start, tiles, m, blocks, v):
    size = v.shape[0]
    nothing = jnp.zeros((8, C), F32)

    def store(block, value):
        lanes = slice(C * block, C * block + C)
        own = value.reshape(size // 2, 16, C).astype(BF16)
        buf[i, 1 + start : 1 + start + size // 2, :, lanes] = own
        if start == 0:
            buf[i, tiles + 1, :, lanes] = jnp.concatenate([value[1], nothing], 0).astype(BF16)
        if start + size // 2 == tiles:
            buf[i, 0, :, lanes] = jnp.concatenate([nothing, value[size - 2]], 0).astype(BF16)

    store(1 + m, v)
    if m == 0:
        store(blocks + 1, shift_up(v))
    if m == blocks - 1:
        store(0, shift_down(v))


def get(ref, i, start, tiles, m):
    return ref[i, start : start + tiles, :, C * m : C * m + C].reshape(tiles // 2, 2, 2, 8, C)


def set_(ref, i, start, tiles, m, v):
    ref[i, start : start + tiles, :, C * m : C * m + C] = v.reshape(tiles, 16, C)


def total(v):
    return jnp.sum(v.reshape(-1, 8, C), axis=0)


def channel(v):
    return jnp.broadcast_to(jnp.sum(v, axis=0, keepdims=True), (8, C))


def loop(count, body, carry=0):
    return lax.fori_loop(0, count, body, carry)


def write_weights(dst, tap):
    for r in range(3):
        for j in range(4):
            for o in range(2):
                s = j - o
                value = tap(r, s).astype(BF16) if 0 <= s <= 2 else jnp.zeros((C, C), BF16)
                row = C * (4 * r + j)
                dst[row : row + C, C * o : C * o + C] = value


def write_weights_back(dst, tap):
    for r in range(3):
        for j in range(4):
            for o in range(2):
                s = j - o
                value = tap(2 - r, 2 - s).astype(BF16) if 0 <= s <= 2 else jnp.zeros((C, C), BF16)
                col = C * (4 * r + j)
                dst[C * o : C * o + C, col : col + C] = value


NN = (((1,), (0,)), ((), ()))
NT = (((1,), (1,)), ((), ()))
TN = (((0,), (0,)), ((), ()))


def dot(a, b, dims=NN):
    return lax.dot_general(a, b, dims, preferred_element_type=F32)


def rows_one(buf, i, q):
    return jnp.concatenate(
        [buf[i, r : r + 16, :, 256 * q : 256 * q + 512].reshape(256, 512) for r in range(3)], 1
    )


def rows_two(buf, first, number):
    return jnp.concatenate(
        [buf[pl.ds(first, number), r : r + 8].reshape(128 * number, 512) for r in range(3)], 1
    )


def by_two(count, work):
    odd = count % 2 == 1

    @pl.when(odd)
    def _():
        work(count - 1, 1, True)

    @pl.when(jnp.logical_not(odd))
    def _():
        work(0, 2, True)

    def step(p, _):
        work(2 * p, 2, False)
        return 0

    lax.fori_loop(jnp.where(odd, 0, 1), count // 2, step, 0)


def conv_all(count, work):
    def step(p, _):
        work(2 * p, 2)
        return 0

    loop(count // 2, step)

    @pl.when(count % 2 == 1)
    def _():
        work(count - 1, 1)


def conv_one(count, pairs, emit, dims=NN):
    def images(first, number):
        for n in range(number):
            for q in range(2):
                value = None
                for buf, weights in pairs:
                    term = dot(rows_one(buf, first + n, q), weights[...], dims)
                    value = term if value is None else value + term
                emit(first + n, q, value)

    conv_all(count, images)


def conv_two(count, pairs, dst, dims=NN):
    def images(first, number):
        value = None
        for buf, weights in pairs:
            term = dot(rows_two(buf, 2 * first, 2 * number), weights[...], dims)
            value = term if value is None else value + term
        dst[pl.ds(2 * first, 2 * number)] = value.reshape(2 * number, 8, 16, 256)

    conv_all((count + 1) // 2, images)


def kernel_grad_one(count, x, d, acc):
    def images(first, number, fresh):
        places = [(first + n, q) for n in range(number) for q in range(2)]
        grads = jnp.concatenate(
            [d[i, 1:17, :, 128 + 256 * q : 384 + 256 * q].reshape(256, 256) for i, q in places], 0
        )
        for r in range(3):
            ins = jnp.concatenate(
                [x[i, r : r + 16, :, 256 * q : 256 * q + 512].reshape(256, 512) for i, q in places],
                0,
            )
            value = dot(ins, grads, TN)
            acc[r] = value if fresh else acc[r] + value

    by_two(count, images)


def kernel_grad_two(count, pairs, acc):
    def images(first, number, fresh):
        at, size = pl.ds(2 * first, 2 * number), 256 * number
        grads = jnp.concatenate([d[at, 1:9, :, 128:384].reshape(size, 256) for _, d in pairs], 0)
        for r in range(3):
            ins = jnp.concatenate([x[at, r : r + 8].reshape(size, 512) for x, _ in pairs], 0)
            value = dot(ins, grads, TN)
            acc[r] = value if fresh else acc[r] + value

    by_two((count + 1) // 2, images)


def grad_tap(acc, r, s):
    return (
        acc[r, C * s : C * s + C, 0:C] + acc[r, C * (s + 1) : C * (s + 1) + C, C : 2 * C]
    )


def statistics(count, z, cells, tiles, chunk, blocks, summed=None):
    def add(i, acc):
        for start in range(0, tiles, chunk):
            for m in range(blocks):
                acc = acc + total(get(z, i, start, chunk, m))
        return acc

    zero = jnp.zeros((8, C), F32)
    mean = channel(loop(count, add, zero) if summed is None else summed) / cells

    def add_square(i, acc):
        for start in range(0, tiles, chunk):
            for m in range(blocks):
                centred = get(z, i, start, chunk, m) - mean
                set_(z, i, start, chunk, m, centred)
                acc = acc + total(centred * centred)
        return acc

    variance = channel(loop(count, add_square, zero)) / cells
    return lax.rsqrt(variance + EPSILON)


def activate(count, zc, s1, s2, pools, inverse, gain, shift, tiles, chunk, blocks, emit):
    scale, offset = 0.5 * gain * inverse, 0.5 * shift

    def step(i, _):
        for start in range(0, tiles, chunk):
            for half in range(blocks // 2):
                sums = []
                for m in (2 * half, 2 * half + 1):
                    centred = get(zc, i, start, chunk, m)
                    h = centred * scale + offset
                    bend = jnp.tanh(h)
                    over, under = 1.0 + bend, 1.0 - bend
                    slope = over * (1.0 + h * under)
                    set_(s1, i, start, chunk, m, slope)
                    if s2 is not None:
                        set_(s2, i, start, chunk, m, over * under * (1.0 - h * bend))
                    sums.append([jnp.sum(v, axis=1) for v in (h * over, slope, slope * centred)])
                pooled, *slopes = (one + two for one, two in zip(*sums))
                for ref, value in zip(pools, slopes):
                    place = i, slice(start // 2, start // 2 + chunk // 2), slice(None), slice(C * half, C * half + C)
                    ref[place] = value.reshape(chunk // 2, 16, C)
                emit(i, start, half, pooled)
        return 0

    loop(count, step)


def pooled_sums(count, pools, up, tiles, blocks):
    def add(i, carry):
        sums = list(carry)
        for half in range(blocks // 2):
            weight = up(i, 0, half, tiles).reshape(tiles // 2, 2, 8, C)
            for n, ref in enumerate(pools):
                value = ref[i, :, :, C * half : C * half + C].reshape(tiles // 2, 2, 8, C)
                sums[n] = sums[n] + total(weight * value)
        return tuple(sums)

    zero = jnp.zeros((8, C), F32)
    return tuple(channel(v) for v in loop(count, add, (zero, zero)))


def first_backward(count, zc, s1, pools, up, dst, gain, inverse, cells, tiles, chunk, blocks):
    one, two = pooled_sums(count, pools, up, tiles, blocks)
    two = two * inverse
    mean_one, mean_two = one / cells, two / cells
    scale = gain * inverse
    offset, tilt = scale * mean_one, scale * mean_two * inverse

    def step(i, _):
        for start in range(0, tiles, chunk):
            for m in range(blocks):
                dy = scale * up(i, start, m // 2, chunk) * get(s1, i, start, chunk, m)
                dz = dy - offset - get(zc, i, start, chunk, m) * tilt
                put(dst, i, start, tiles, m, blocks, dz.reshape(-1, 8, C))
        return 0

    loop(count, step)
    return mean_one, mean_two, one, two


def clear_odd(count, buffers):
    @pl.when(count % 2 == 1)
    def _():
        for buf in buffers:
            buf[count] = jnp.zeros(buf.shape[1:], buf.dtype)


def mix_taps(weight, src, dst):
    for g in range(0, C, MIX_ROWS):
        rows = slice(g, g + MIX_ROWS)
        values = [src(f, rows) for f in range(9)]
        for q in range(9):
            acc = weight(q, 0) * values[0]
            for f in range(1, 9):
                acc = acc + weight(q, f) * values[f]
            dst(q, rows, acc)


def transform(acc, kernel, outer, inner, taps, g_low, t_one, t_two, fast):
    for f in range(9):
        g_low[:, C * f : C * f + C] = grad_tap(acc, f // 3, f % 3).astype(BF16)
    t_one[...] = dot(inner[...].astype(BF16), g_low[...])

    def write(q, rows, value):
        t_two[q, rows, :] = value

    mix_taps(
        lambda q, f: taps[q, f], lambda f, rows: t_one[rows, C * f : C * f + C], write
    )
    turned = dot(t_two[...].reshape(9 * C, C).astype(BF16), outer[...].astype(BF16), NT)
    fast[...] = kernel[...] - STEP_RATE * turned.reshape(9, C, C)


def transform_back(acc, outer, inner, taps, g_low, t_one, t_two, d_low, e, w, payload, u):
    for q in range(9):
        grad = grad_tap(acc, q // 3, q % 3)
        payload[C * q : C * q + C, :] = grad
        d_low[C * q : C * q + C, :] = (-STEP_RATE * grad).astype(BF16)
    e[...] = dot(d_low[...], outer[...].astype(BF16)).reshape(9, C, C)
    payload[AT_OUTER:AT_INNER, :] = dot(
        d_low[...], t_two[...].reshape(9 * C, C).astype(BF16), TN
    )

    def write(f, rows, value):
        w[rows, C * f : C * f + C] = value

    mix_taps(lambda f, q: taps[q, f], lambda q, rows: e[q, rows, :], write)
    w_low = w[...].astype(BF16)
    payload[AT_INNER:AT_SMALL, :] = dot(w_low, g_low[...], NT)
    u[...] = dot(inner[...].astype(BF16), w_low, TN)
    sums = []
    for first in range(0, 9, 3):
        parts = [jnp.zeros((8, C), F32)] * 27
        for g in range(0, C, 8):
            ones = [t_one[g : g + 8, C * f : C * f + C] for f in range(9)]
            for n in range(27):
                if n % 9 == 0:
                    grad = e[first + n // 9, g : g + 8, :]
                parts[n] = parts[n] + grad * ones[n % 9]
        sums += parts
    sums = jnp.concatenate([jnp.sum(v, axis=0, keepdims=True) for v in sums], 0)
    sums = jnp.concatenate([jnp.sum(sums, axis=1, keepdims=True), jnp.zeros((7, 1), F32)], 0)
    spread = jnp.broadcast_to(sums, (88, C))
    row = lax.broadcasted_iota(jnp.int32, (88, C), 0)
    lane = lax.broadcasted_iota(jnp.int32, (88, C), 1)
    spread = jnp.where(row % 9 == lane, spread, 0.0)
    chosen = lax.broadcasted_iota(jnp.int32, (16, 88), 1) // 9 == lax.broadcasted_iota(
        jnp.int32, (16, 88), 0
    )
    payload[AT_SMALL : AT_SMALL + 16, :] = lax.dot_general(
        chosen.astype(F32), spread, NN, precision=lax.Precision.HIGHEST, preferred_element_type=F32
    )


def second_sums(count, c, zc, s1, up, inverse, cells, tiles, chunk, blocks):
    def add(i, carry):
        one, two, three = carry
        for start in range(0, tiles, chunk):
            for m in range(blocks):
                value = get(c, i, start, chunk, m)
                dy = up(i, start, m // 2, chunk) * get(s1, i, start, chunk, m)
                one = one + total(value)
                two = two + total(value * get(zc, i, start, chunk, m))
                three = three + total(value * dy)
        return one, two, three

    zero = jnp.zeros((8, C), F32)
    one, two, three = loop(count, add, (zero, zero, zero))
    return channel(one) / cells, channel(two) * inverse / cells, channel(three) / cells


def second_turn(count, c, zc, s1, s2, up, means, gain, inverse, emit, tiles, chunk, blocks):
    mean_c, mean_cz, _ = means
    scale, tilt = gain * inverse, mean_cz * inverse

    def step(i, carry):
        one, two = carry
        for start in range(0, tiles, chunk):
            for half in range(blocks // 2):
                pooled = None
                weight = scale * up(i, start, half, chunk)
                for m in (2 * half, 2 * half + 1):
                    centred = get(zc, i, start, chunk, m)
                    turned = get(c, i, start, chunk, m) - mean_c - centred * tilt
                    cy = turned * (weight * get(s2, i, start, chunk, m))
                    set_(s2, i, start, chunk, m, cy)
                    one = one + total(cy)
                    two = two + total(cy * centred)
                    if emit is not None:
                        part = jnp.sum(turned * get(s1, i, start, chunk, m), axis=1)
                        pooled = part if pooled is None else pooled + part
                if emit is not None:
                    emit(i, start, half, 0.5 * scale * pooled)
        return one, two

    zero = jnp.zeros((8, C), F32)
    one, two = loop(count, step, (zero, zero))
    return channel(one), channel(two) * inverse


def second_close(
    count, c, zc, s1, t_buf, up, extra, dst, means, sums, first_means, gain, inverse, cells, tiles, chunk, blocks
):
    mean_c, mean_cz, mean_cdy = means
    mean_dy, mean_dyz = first_means
    mean_cy, mean_cyz = sums[0] / cells, sums[1] / cells
    scale = gain * inverse
    mean_cw = mean_cdy - mean_c * mean_dy - mean_cz * mean_dyz
    mean_z = gain * mean_cy - scale * (mean_c * mean_dyz + mean_dy * mean_cz)
    mean_zz = gain * mean_cyz - 2.0 * scale * mean_cz * mean_dyz
    alpha = inverse * gain
    beta = scale * inverse * mean_dyz
    gamma = scale * inverse * mean_cz
    delta = inverse * mean_z
    epsilon = inverse * inverse * (mean_zz + scale * mean_cw)

    def step(i, _):
        for start in range(0, tiles, chunk):
            for m in range(blocks):
                weight = -gamma * up(i, start, m // 2, chunk)
                if extra is not None:
                    weight = weight + alpha * extra(i, start, m // 2, chunk)
                value = (
                    alpha * get(t_buf, i, start, chunk, m)
                    + weight * get(s1, i, start, chunk, m)
                    - beta * get(c, i, start, chunk, m)
                    - epsilon * get(zc, i, start, chunk, m)
                    - delta
                )
                put(dst, i, start, tiles, m, blocks, value.reshape(-1, 8, C))
        return 0

    loop(count, step)
    return sums[1] + inverse * cells * mean_cw


def image_grads(count, pairs, dst, wide):
    def emit(i, q, value):
        for o in range(2):
            v = value[:, C * o : C * o + C].reshape(16, 2, 8, C)
            for b in range(2):
                wide[16 * b : 16 * b + 16, pl.ds(2 * q + o, 8, stride=4), :] = v[:, b]
        if q == 1:
            dst[i] = wide[...].astype(BF16)

    conv_one(count, pairs, emit, NT)

    def dead(i, _):
        dst[i] = jnp.zeros(dst.shape[1:], BF16)
        return 0

    lax.fori_loop(count, dst.shape[0], dead, 0)


def query_grad_kernel(count, grads, weights, after, dst, zeros, wide):
    zeros[...] = jnp.zeros(zeros.shape, F32)
    image_grads(count[0], [(grads, weights)], dst, wide)


def support_grad_kernel(
    count, inner_grads, inner_weights, grads, kernel, after, dst, zeros, wide, weights
):
    zeros[...] = jnp.zeros(zeros.shape, F32)
    write_weights_back(weights, lambda r, s: kernel[3 * r + s])
    image_grads(count[0], [(inner_grads, inner_weights), (grads, weights)], dst, wide)


def run_image_grads(kernel, name, shape, after, operands, scratch):
    vmem = pl.BlockSpec(memory_space=pltpu.VMEM)
    images = operands[1].shape[0]
    convs = (len(operands) - 1) // 2
    return pl.pallas_call(
        kernel,
        out_shape=(jax.ShapeDtypeStruct(shape, BF16), pltpu.VMEM((8, C), F32)),
        in_specs=[pl.BlockSpec(memory_space=pltpu.SMEM)]
        + [vmem] * (len(operands) - 1)
        + [pl.BlockSpec(memory_space=pl.ANY)],
        out_specs=(vmem, vmem),
        scratch_shapes=[pltpu.VMEM((32, 32, C), F32)] + scratch,
        compiler_params=pltpu.CompilerParams(vmem_limit_bytes=VMEM_SMALL),
        cost_estimate=pl.CostEstimate(
            flops=2 * images * convs * 1024 * 1536 * C,
            bytes_accessed=images * (convs + 1) * 32 * 32 * C * 2,
            transcendentals=0,
        ),
        name=name,
    )(*operands, after)


SCALARS = ["support_count", "query_count", "taps_one", "taps_two"]
NORMS = ["gain_one", "shift_one", "gain_two", "shift_two"]
AT_OUTER, AT_INNER, AT_SMALL, AT_GAIN, HALF_ROWS = 9 * C, 10 * C, 11 * C, 11 * C + 16, 11 * C + 32
QUARTER = HALF_ROWS // 4
FETCHED = [
    "kernel_one",
    "support",
    "gain_one",
    "shift_one",
    "gain_two",
    "shift_two",
    "kernel_two",
    "target",
    "inner_two",
    "outer_two",
    "inner_one",
    "outer_one",
    "query",
    "cotangent",
]
HELD = ["query_output", "grad_q", "back_q", "grad_s", "back_s", "grad_e"]
KEPT = [f"keep_{at}" for at in range(4)]
GIVEN = [f"send_{at}" for at in range(4)]


def scratch_of(s_cap, q_cap):
    def operand(count, tiles, blocks):
        return pltpu.VMEM((count, tiles + 2, 16, C * (blocks + 2)), BF16)

    def plain(count, tiles, blocks):
        return pltpu.VMEM((count, tiles, 16, C * blocks), F32)

    weights = pltpu.VMEM((1536, 256), BF16)
    weights_back = pltpu.VMEM((256, 1536), BF16)
    square = pltpu.VMEM((C, 9 * C), F32)
    square_low = pltpu.VMEM((C, 9 * C), BF16)
    stack = pltpu.VMEM((9, C, C), F32)
    s_even, q_even = s_cap + s_cap % 2, q_cap + q_cap % 2
    return dict(
        wide=pltpu.VMEM((32, 32, C), F32),
        xs=operand(s_cap, 16, 4),
        xq=operand(q_cap, 16, 4),
        ds=operand(s_cap, 16, 4),
        dq=operand(q_cap, 16, 4),
        zs=plain(s_cap, 16, 4),
        s1s=plain(s_cap, 16, 4),
        s2s=plain(s_cap, 16, 4),
        zq=plain(q_cap, 16, 4),
        s1q=plain(q_cap, 16, 4),
        hs=operand(s_even, 8, 2),
        ds2=operand(s_even, 8, 2),
        hq=operand(q_even, 8, 2),
        dq2=operand(q_even, 8, 2),
        zs2=plain(s_even, 8, 2),
        s1s2=plain(s_even, 8, 2),
        s2s2=plain(s_even, 8, 2),
        dhs=plain(s_even, 8, 2),
        chs_back=plain(s_even, 8, 2),
        zq2=plain(q_even, 8, 2),
        s1q2=plain(q_even, 8, 2),
        dhq=plain(q_even, 8, 2),
        p1s=plain(s_cap, 8, 2),
        p2s=plain(s_cap, 8, 2),
        p1s2=plain(s_cap, 4, 1),
        p2s2=plain(s_cap, 4, 1),
        p1q=plain(q_cap, 8, 2),
        p2q=plain(q_cap, 8, 2),
        p1q2=plain(q_cap, 4, 1),
        p2q2=plain(q_cap, 4, 1),
        sums=pltpu.VMEM((3, 8, C), F32),
        w_a=weights,
        w_b=weights,
        w_c=weights,
        b_k2=weights_back,
        b_f1=weights_back,
        b_f2=weights_back,
        b_u1=weights_back,
        b_u2=weights_back,
        acc=pltpu.VMEM((3, 512, 256), F32),
        g_one=square_low,
        g_two=square_low,
        t1_one=square,
        t1_two=square,
        t2_one=stack,
        t2_two=stack,
        f_one=stack,
        f_two=stack,
        d_low=pltpu.VMEM((9 * C, C), BF16),
        e_buf=stack,
        w_buf=square,
        u_buf=square,
        payload=pltpu.VMEM((2, HALF_ROWS, C), F32),
        gain_one_v=pltpu.VMEM((1, C), F32),
        shift_one_v=pltpu.VMEM((1, C), F32),
        gain_two_v=pltpu.VMEM((1, C), F32),
        shift_two_v=pltpu.VMEM((1, C), F32),
        output_v=pltpu.VMEM((q_cap, 8, 8, C), BF16),
        support_v=pltpu.VMEM((s_cap, 32, 32, C), BF16),
        query_v=pltpu.VMEM((q_cap, 32, 32, C), BF16),
        target_v=pltpu.VMEM((s_cap, 8, 8, C), BF16),
        cotangent_v=pltpu.VMEM((q_cap, 8, 8, C), BF16),
        kernel_one_v=stack,
        kernel_two_v=stack,
        inner_one_v=pltpu.VMEM((C, C), F32),
        outer_one_v=pltpu.VMEM((C, C), F32),
        inner_two_v=pltpu.VMEM((C, C), F32),
        outer_two_v=pltpu.VMEM((C, C), F32),
        fetch_sem=pltpu.SemaphoreType.DMA((len(FETCHED),)),
        send_sem=pltpu.SemaphoreType.DMA((len(HELD),)),
    )


def task_kernel(names, *refs):
    k = SimpleNamespace(**dict(zip(names, refs)))
    fetches = {}
    for n, name in enumerate(FETCHED):
        fetches[name] = pltpu.make_async_copy(getattr(k, name), getattr(k, name + "_v"), k.fetch_sem.at[n])
        setattr(k, name, getattr(k, name + "_v"))
    for name in FETCHED[:6]:
        fetches[name].start()
    sent = []

    def ready(*wanted):
        for name in wanted:
            fetches[name].wait()

    def send(name, source):
        copy = pltpu.make_async_copy(source, getattr(k, name), k.send_sem.at[HELD.index(name)])
        copy.start()
        sent.append(copy)

    def close_layer(layer, gain_grad, shift_grad):
        pay = k.payload.at[layer]
        pay[AT_GAIN : AT_GAIN + 2, :] = jnp.concatenate([gain_grad[0:1], shift_grad[0:1]], 0)
        pay[AT_GAIN + 2 :, :] = jnp.zeros((HALF_ROWS - AT_GAIN - 2, C), F32)
        half, place = my_place()
        for at in range(4):
            rows = pl.ds(pl.multiple_of((place ^ at) * QUARTER, 8), QUARTER)
            for kept in (True, False):
                target = getattr(k, f"keep_{at}" if kept else f"send_{at}")

                @pl.when(half == (layer if kept else 1 - layer))
                def _(target=target, rows=rows):
                    target[...] = pay[rows, :]

    ns, nq = k.support_count[0], k.query_count[0]
    ns_f, nq_f = ns.astype(F32), nq.astype(F32)
    pay_one, pay_two = k.payload.at[0], k.payload.at[1]
    k.cs, k.es, k.cs2, k.es2, k.chs = k.zq, k.xq, k.zq2, k.hq, k.dq2
    one = dict(tiles=16, chunk=4, blocks=4)
    two = dict(tiles=8, chunk=4, blocks=2)
    wide = k.wide

    def load_images(count, src, dst):
        def image(i, _):
            wide[...] = src[i].astype(F32)
            for m in range(4):
                v = wide[:, pl.ds(m, 8, stride=4), :].reshape(2, 16, 1, 8, C)
                v = jnp.concatenate([v[0], v[1]], 1)
                put(dst, i, 0, 16, m, 4, v.reshape(32, 8, C))
            return 0

        loop(count, image)

    def keep(dst, terms):
        k.sums[...] = jnp.zeros(k.sums.shape, F32)

        def emit(i, q, value):
            dst[i, :, :, 256 * q : 256 * q + 256] = value.reshape(16, 16, 256)
            added = None
            for o in range(2):
                block = value[:, C * o : C * o + C].reshape(8, 2, 2, 8, C)
                parts = [total(term) for term in terms(i, 2 * q + o, block)]
                added = parts if added is None else [v + w for v, w in zip(added, parts)]
            for n, part in enumerate(added):
                k.sums[n] += part

        return emit

    def alone(i, m, block):
        return [block]

    def pool_to(dst):
        def emit(i, start, half, pooled):
            put(dst, i, start // 2, 8, half, 2, (0.25 * pooled).reshape(-1, 8, C))

        return emit

    def up_from(ref):
        def up(i, start, half, chunk):
            number = chunk // 2
            v = ref[i, start // 2 : start // 2 + number, :, C * half : C * half + C]
            return 0.125 * v.reshape(number, 1, 2, 8, C)

        return up

    def up_from_rows(ref, scale):
        def up(i, start, half, chunk):
            number = chunk // 2
            v = ref[i].astype(F32) * scale
            parts = [v[at : at + number].reshape(number, 1, 1, 8, C) for at in (start // 2, 4 + start // 2)]
            return jnp.concatenate(parts, 2)

        return up

    def tap_of(ref):
        return lambda r, s: ref[3 * r + s]

    def tap_wide(ref):
        return lambda r, s: ref[:, C * (3 * r + s) : C * (3 * r + s) + C]

    pools_one, pools_two = (k.p1s, k.p2s), (k.p1s2, k.p2s2)
    pools_q1, pools_q2 = (k.p1q, k.p2q), (k.p1q2, k.p2q2)

    cells_one, cells_two = ns_f * 1024.0, ns_f * 256.0
    ready("kernel_one")
    write_weights(k.w_a, tap_of(k.kernel_one))
    ready("support", *NORMS)
    for name in FETCHED[6:]:
        fetches[name].start()
    gain_one, shift_one, gain_two, shift_two = (
        jnp.broadcast_to(getattr(k, name)[...], (8, C)) for name in NORMS
    )
    load_images(ns, k.support, k.xs)
    conv_one(ns, [(k.xs, k.w_a)], keep(k.zs, alone))
    stats_one = statistics(ns, k.zs, cells_one, summed=k.sums[0], **one)
    activate(ns, k.zs, k.s1s, k.s2s, pools_one, stats_one, gain_one, shift_one, emit=pool_to(k.hs), **one)
    clear_odd(ns, [k.hs, k.ds2])
    ready("kernel_two", "target", "inner_two", "outer_two")
    write_weights(k.w_b, tap_of(k.kernel_two))
    conv_two(ns, [(k.hs, k.w_b)], k.zs2)
    stats_two = statistics(ns, k.zs2, cells_two, **two)
    activate(ns, k.zs2, k.s1s2, k.s2s2, pools_two, stats_two, gain_two, shift_two, emit=lambda *a: None, **two)

    up_two = up_from_rows(k.target, 1.0 / (512.0 * ns_f))
    mean_dy2, mean_dyz2, _, _ = first_backward(
        ns, k.zs2, k.s1s2, pools_two, up_two, k.ds2, gain_two, stats_two, cells_two, **two
    )
    kernel_grad_two(ns, [(k.hs, k.ds2)], k.acc)
    transform(
        k.acc, k.kernel_two, k.outer_two, k.inner_two, k.taps_two, k.g_two, k.t1_two, k.t2_two, k.f_two
    )
    write_weights_back(k.b_k2, tap_of(k.kernel_two))
    conv_two(ns, [(k.ds2, k.b_k2)], k.dhs, NT)
    up_one = up_from(k.dhs)
    mean_dy1, mean_dyz1, _, _ = first_backward(
        ns, k.zs, k.s1s, pools_one, up_one, k.ds, gain_one, stats_one, cells_one, **one
    )
    send("grad_s", k.ds)
    ready("inner_one", "outer_one", "query", "cotangent")
    kernel_grad_one(ns, k.xs, k.ds, k.acc)
    transform(
        k.acc, k.kernel_one, k.outer_one, k.inner_one, k.taps_one, k.g_one, k.t1_one, k.t2_one, k.f_one
    )

    cells_q1, cells_q2 = nq_f * 1024.0, nq_f * 256.0
    write_weights(k.w_a, tap_of(k.f_one))
    load_images(nq, k.query, k.xq)
    conv_one(nq, [(k.xq, k.w_a)], keep(k.zq, alone))
    stats_q1 = statistics(nq, k.zq, cells_q1, summed=k.sums[0], **one)
    activate(nq, k.zq, k.s1q, None, pools_q1, stats_q1, gain_one, shift_one, emit=pool_to(k.hq), **one)
    clear_odd(nq, [k.hq, k.dq2])
    write_weights(k.w_c, tap_of(k.f_two))
    conv_two(nq, [(k.hq, k.w_c)], k.zq2)
    stats_q2 = statistics(nq, k.zq2, cells_q2, **two)

    def produce(i, start, half, pooled):
        v = (0.25 * pooled).astype(BF16)
        at, number = start // 2, v.shape[0]
        k.output_v[i, at : at + number] = v[:, 0]
        k.output_v[i, 4 + at : 4 + at + number] = v[:, 1]

    activate(nq, k.zq2, k.s1q2, None, pools_q2, stats_q2, gain_two, shift_two, emit=produce, **two)

    def dead(i, _):
        k.output_v[i] = jnp.zeros(k.output_v.shape[1:], BF16)
        return 0

    lax.fori_loop(nq, k.output_v.shape[0], dead, 0)
    send("query_output", k.output_v)

    _, _, db2, dg2 = first_backward(
        nq, k.zq2, k.s1q2, pools_q2, up_from_rows(k.cotangent, 0.125 / nq_f), k.dq2, gain_two, stats_q2, cells_q2, **two
    )
    kernel_grad_two(nq, [(k.hq, k.dq2)], k.acc)
    transform_back(
        k.acc, k.outer_two, k.inner_two, k.taps_two, k.g_two, k.t1_two, k.t2_two, k.d_low, k.e_buf, k.w_buf,
        pay_two, k.u_buf,
    )
    write_weights_back(k.b_f2, tap_of(k.f_two))
    write_weights(k.w_c, tap_wide(k.u_buf))
    write_weights_back(k.b_u2, tap_wide(k.u_buf))
    conv_two(nq, [(k.dq2, k.b_f2)], k.dhq, NT)
    _, _, db1, dg1 = first_backward(
        nq, k.zq, k.s1q, pools_q1, up_from(k.dhq), k.dq, gain_one, stats_q1, cells_q1, **one
    )
    send("grad_q", k.dq)
    kernel_grad_one(nq, k.xq, k.dq, k.acc)
    transform_back(
        k.acc, k.outer_one, k.inner_one, k.taps_one, k.g_one, k.t1_one, k.t2_one, k.d_low, k.e_buf, k.w_buf,
        pay_one, k.u_buf,
    )
    write_weights_back(k.b_f1, tap_of(k.f_one))
    send("back_q", k.b_f1)
    write_weights(k.w_a, tap_wide(k.u_buf))
    write_weights_back(k.b_u1, tap_wide(k.u_buf))
    send("back_s", k.b_u1)

    clear_odd(ns, [k.chs, k.es2])

    def second_terms(i, m, block):
        dy = up_one(i, 0, m // 2, 16) * get(k.s1s, i, 0, 16, m)
        return [block, block * get(k.zs, i, 0, 16, m), block * dy]

    conv_one(ns, [(k.xs, k.w_a)], keep(k.cs, second_terms))
    means_one = tuple(channel(k.sums[n]) / cells_one for n in range(3))
    means_one = means_one[0], means_one[1] * stats_one, means_one[2]
    turn_one = second_turn(
        ns, k.cs, k.zs, k.s1s, k.s2s, up_one, means_one, gain_one, stats_one, pool_to(k.chs), **one
    )
    conv_two(ns, [(k.chs, k.w_b), (k.hs, k.w_c)], k.cs2)
    means_two = second_sums(ns, k.cs2, k.zs2, k.s1s2, up_two, stats_two, cells_two, **two)
    turn_two = second_turn(
        ns, k.cs2, k.zs2, k.s1s2, k.s2s2, up_two, means_two, gain_two, stats_two, None, **two
    )
    extra_g2 = second_close(
        ns, k.cs2, k.zs2, k.s1s2, k.s2s2, up_two, None, k.es2, means_two, turn_two, (mean_dy2, mean_dyz2),
        gain_two, stats_two, cells_two, **two,
    )
    conv_two(ns, [(k.ds2, k.b_u2), (k.es2, k.b_k2)], k.chs_back, NT)
    kernel_grad_two(ns, [(k.chs, k.ds2), (k.hs, k.es2)], k.acc)
    for f in range(9):
        pay_two[C * f : C * f + C, :] += grad_tap(k.acc, f // 3, f % 3)
    close_layer(1, dg2 + extra_g2, db2 + turn_two[0])
    up_back = up_from(k.chs_back)
    more = pooled_sums(ns, pools_one, up_back, 16, 4)
    turn_one = (turn_one[0] + more[0], turn_one[1] + more[1] * stats_one)
    extra_g1 = second_close(
        ns, k.cs, k.zs, k.s1s, k.s2s, up_one, up_back, k.es, means_one, turn_one, (mean_dy1, mean_dyz1),
        gain_one, stats_one, cells_one, **one,
    )
    send("grad_e", k.es.at[pl.ds(0, k.xs.shape[0])])
    kernel_grad_one(ns, k.xs, k.es, k.acc)
    for f in range(9):
        pay_one[C * f : C * f + C, :] += grad_tap(k.acc, f // 3, f % 3)
    close_layer(0, dg1 + extra_g1, db1 + turn_one[0])
    for copy in sent:
        copy.wait()


def run_task(values):
    s_cap, q_cap = values["support"].shape[0], values["query"].shape[0]
    scratch = scratch_of(s_cap, q_cap)
    vmem = pl.BlockSpec(memory_space=pltpu.VMEM)
    smem = pl.BlockSpec(memory_space=pltpu.SMEM)
    anywhere = pl.BlockSpec(memory_space=pl.ANY)

    def operand(count):
        return jax.ShapeDtypeStruct((count, 18, 16, 6 * C), BF16)

    back = jax.ShapeDtypeStruct((256, 1536), BF16)
    rows = pltpu.VMEM((QUARTER, C), F32)
    inputs = SCALARS + FETCHED
    outputs = HELD + KEPT + GIVEN
    results = pl.pallas_call(
        partial(task_kernel, inputs + outputs + list(scratch)),
        out_shape=(
            jax.ShapeDtypeStruct(values["cotangent"].shape, BF16),
            operand(q_cap),
            back,
            operand(s_cap),
            back,
            operand(s_cap),
            *[rows] * 8,
        ),
        in_specs=[smem] * len(SCALARS) + [anywhere] * len(FETCHED),
        out_specs=[anywhere] * len(HELD) + [vmem] * 8,
        scratch_shapes=list(scratch.values()),
        compiler_params=pltpu.CompilerParams(vmem_limit_bytes=VMEM_BYTES),
        name="task",
    )(*[values[name] for name in inputs])
    return dict(zip(outputs, results))


def swap(value, mask):
    extent = lax.axis_size(AXES)
    return lax.ppermute(value, AXES, [(place, place ^ mask) for place in range(extent)])


def sum_quarters(kept, sent, first, second):
    extent = lax.axis_size(AXES)
    come = {n: swap(sent[n], 1) for n in (3, 1, 2, 0)}
    mine = {n: kept[n] + come[n] for n in (3, 1, 2, 0)}
    terms = {n: swap(mine[n], 2 * n) for n in (3, 1, 2)}
    one, zeros = first(come[0][0:8])
    part = mine[0] + terms[3] + terms[1] + terms[2] + zeros[0:1]
    mask, two = 8, None
    while mask < extent:
        passed = swap(part, mask)
        if 2 * mask >= extent:
            two, zeros = second(part[0:8])
            passed = passed + zeros[0:1]
        part = part + passed
        mask *= 2
    if two is None:
        two, _ = second(part[0:8])
    quarters = [part] + [swap(part, 2 * n) for n in (1, 2, 3)]
    return one, two, quarters, [swap(quarter, 1) for quarter in quarters]


def sum_plain(kept, sent, first, second):
    half, at = my_place()
    whole = jnp.stack([*kept, *sent]).reshape(2, 4, QUARTER, C)
    whole = jnp.where(half == 0, whole, whole[::-1])
    order = at ^ jnp.arange(4)
    whole = lax.psum(jnp.take(whole, order, axis=1), AXES)
    whole = jnp.take(jnp.where(half == 0, whole, whole[::-1]), order, axis=1)
    results = first(whole)[0], second(whole)[0]
    return *results, list(whole[0]), list(whole[1])


LAYER = ["outer", "inner", "taps"]


def my_place():
    me = lax.axis_index(AXES)
    return me & 1, (me >> 1) & 3


def finish_kernel(*refs):
    pieces, refs = refs[:8], refs[8:]
    factors, refs = refs[:6], refs[6:]
    results, refs = refs[:12], refs[12:]
    rest, kernel_sem = refs
    half, at = my_place()
    whole = AT_OUTER // QUARTER
    last = AT_OUTER - whole * QUARTER
    for n, piece in enumerate(pieces):
        quarter = at ^ (n % 4)
        for layer in range(2):
            kernel = results[6 * layer]
            own = half == layer if n < 4 else half != layer

            @pl.when(own & (quarter < whole))
            def _(piece=piece, kernel=kernel, quarter=quarter, layer=layer):
                start = pl.multiple_of(quarter * QUARTER, 8)
                pltpu.make_async_copy(
                    piece, kernel.at[pl.ds(start, QUARTER)], kernel_sem.at[layer]
                ).start()

            @pl.when(own & (quarter == whole))
            def _(piece=piece, kernel=kernel, layer=layer):
                rest[layer] = piece[last:QUARTER, :]
                pltpu.make_async_copy(
                    piece.at[pl.ds(0, last)], kernel.at[pl.ds(whole * QUARTER, last)], kernel_sem.at[layer]
                ).start()

    for layer in range(2):
        kernel, gain, shift, outer, inner, taps = results[6 * layer : 6 * layer + 6]
        base = AT_GAIN - AT_OUTER
        gain[...] = rest[layer, base : base + 1, :]
        shift[...] = rest[layer, base + 1 : base + 2, :]
        for start, size, factor, result in zip(
            (0, C, 2 * C), (C, C, 9), factors[3 * layer : 3 * layer + 3], (outer, inner, taps)
        ):
            row = lax.broadcasted_iota(jnp.int32, (size, size), 0)
            column = lax.broadcasted_iota(jnp.int32, (size, size), 1)
            unit = jnp.where(row == column, 1.0, 0.0)
            value = rest[layer, start : start + size, :size]
            result[...] = value + 2.0 * PENALTY * (factor[...] - unit)
    for layer in range(2):
        kernel = results[6 * layer]
        pltpu.make_async_copy(kernel, kernel, kernel_sem.at[layer]).wait()


def run_finish(pieces, factors):
    vmem = pl.BlockSpec(memory_space=pltpu.VMEM)
    anywhere = pl.BlockSpec(memory_space=pl.ANY)

    def shape(*dims):
        return jax.ShapeDtypeStruct(dims, F32)

    layer = [shape(9 * C, C), shape(1, C), shape(1, C), shape(C, C), shape(C, C), shape(9, 9)]
    return pl.pallas_call(
        finish_kernel,
        out_shape=layer * 2,
        in_specs=[vmem] * 14,
        out_specs=([anywhere] + [vmem] * 5) * 2,
        scratch_shapes=[
            pltpu.VMEM((2, HALF_ROWS - AT_OUTER, C), F32),
            pltpu.SemaphoreType.DMA((2,)),
        ],
        compiler_params=pltpu.CompilerParams(vmem_limit_bytes=VMEM_SMALL),
        name="finish",
    )(*pieces, *factors)


def body(
    support_images,
    query_images,
    support_target,
    query_cotangent,
    support_count,
    query_count,
    kernel_one,
    kernel_two,
    gain_one,
    shift_one,
    gain_two,
    shift_two,
    outer_one,
    inner_one,
    taps_one,
    outer_two,
    inner_two,
    taps_two,
):
    shared = dict(
        taps_one=taps_one,
        taps_two=taps_two,
        kernel_one=kernel_one.reshape(9, C, C),
        kernel_two=kernel_two.reshape(9, C, C),
        gain_one=gain_one.reshape(1, C),
        shift_one=shift_one.reshape(1, C),
        gain_two=gain_two.reshape(1, C),
        shift_two=shift_two.reshape(1, C),
        outer_one=outer_one,
        inner_one=inner_one,
        outer_two=outer_two,
        inner_two=inner_two,
    )
    tasks = range(support_images.shape[0])
    results = [
        run_task(
            dict(
                shared,
                support_count=support_count[task : task + 1],
                query_count=query_count[task : task + 1],
                support=support_images[task],
                query=query_images[task],
                target=support_target[task],
                cotangent=query_cotangent[task],
            )
        )
        for task in tasks
    ]

    def query_grads(after):
        done = [
            run_image_grads(
                query_grad_kernel,
                "query_grad",
                query_images.shape[1:],
                after,
                [query_count[task : task + 1], results[task]["grad_q"], results[task]["back_q"]],
                [],
            )
            for task in tasks
        ]
        return jnp.stack([value for value, _ in done]), sum(zeros for _, zeros in done)

    def support_grads(after):
        done = [
            run_image_grads(
                support_grad_kernel,
                "support_grad",
                support_images.shape[1:],
                after,
                [
                    support_count[task : task + 1],
                    *[results[task][name] for name in ("grad_s", "back_s", "grad_e")],
                    shared["kernel_one"],
                ],
                [pltpu.VMEM((256, 1536), BF16)],
            )
            for task in tasks
        ]
        return jnp.stack([value for value, _ in done]), sum(zeros for _, zeros in done)

    kept = [sum(result[name] for result in results) for name in KEPT]
    sent = [sum(result[name] for result in results) for name in GIVEN]
    extent = lax.axis_size(AXES)
    if extent < 8 or extent & (extent - 1):
        summed = sum_plain(kept, sent, query_grads, support_grads)
    else:
        summed = sum_quarters(kept, sent, query_grads, support_grads)
    query_grad, support_grad, mine, others = summed
    factors = [outer_one, inner_one, taps_one, outer_two, inner_two, taps_two]
    last = run_finish([*mine, *others], factors)
    return (
        jnp.stack([result["query_output"] for result in results]),
        support_grad,
        query_grad,
        last[0].reshape(3, 3, C, C),
        last[6].reshape(3, 3, C, C),
        *[last[at].reshape(C) for at in (1, 2, 7, 8)],
        *last[3:6],
        *last[9:12],
    )


def solution(mesh):
    split = P(("tasks", "group"))
    return jax.shard_map(
        body,
        mesh=mesh,
        in_specs=(split,) * 6 + (P(),) * 12,
        out_specs=(split,) * 3 + (P(),) * 12,
        check_vma=False,
    )
```

```python
from functools import partial
from types import SimpleNamespace

import jax
import jax.numpy as jnp
from jax import lax
from jax.experimental import pallas as pl
from jax.experimental.pallas import tpu as pltpu
from jax.sharding import PartitionSpec as P

STEP_RATE = 0.01
PENALTY = 1.0
EPSILON = 1e-05
C = 128
F32 = jnp.float32
BF16 = jnp.bfloat16
VMEM_BYTES = 57 << 20
VMEM_SMALL = 24 << 20
MIX_ROWS = 64
AXES = ("tasks", "group")


def shift_down(v):
    place = lax.broadcasted_iota(jnp.int32, v.shape, v.ndim - 2)
    return jnp.where(place == 0, 0.0, pltpu.roll(v, 1, v.ndim - 2))


def shift_up(v):
    place = lax.broadcasted_iota(jnp.int32, v.shape, v.ndim - 2)
    return jnp.where(place == 7, 0.0, pltpu.roll(v, 7, v.ndim - 2))


def put(buf, i, start, tiles, m, blocks, v):
    size = v.shape[0]
    nothing = jnp.zeros((8, C), F32)

    def store(block, value):
        lanes = slice(C * block, C * block + C)
        own = value.reshape(size // 2, 16, C).astype(BF16)
        buf[i, 1 + start : 1 + start + size // 2, :, lanes] = own
        if start == 0:
            buf[i, tiles + 1, :, lanes] = jnp.concatenate([value[1], nothing], 0).astype(BF16)
        if start + size // 2 == tiles:
            buf[i, 0, :, lanes] = jnp.concatenate([nothing, value[size - 2]], 0).astype(BF16)

    store(1 + m, v)
    if m == 0:
        store(blocks + 1, shift_up(v))
    if m == blocks - 1:
        store(0, shift_down(v))


def get(ref, i, start, tiles, m):
    return ref[i, start : start + tiles, :, C * m : C * m + C].reshape(tiles // 2, 2, 2, 8, C)


def set_(ref, i, start, tiles, m, v):
    ref[i, start : start + tiles, :, C * m : C * m + C] = v.reshape(tiles, 16, C)


def total(v):
    return jnp.sum(v.reshape(-1, 8, C), axis=0)


def channel(v):
    return jnp.broadcast_to(jnp.sum(v, axis=0, keepdims=True), (8, C))


def loop(count, body, carry=0):
    return lax.fori_loop(0, count, body, carry)


def write_weights(dst, tap):
    for r in range(3):
        for j in range(4):
            for o in range(2):
                s = j - o
                value = tap(r, s).astype(BF16) if 0 <= s <= 2 else jnp.zeros((C, C), BF16)
                row = C * (4 * r + j)
                dst[row : row + C, C * o : C * o + C] = value


def write_weights_back(dst, tap):
    for r in range(3):
        for j in range(4):
            for o in range(2):
                s = j - o
                value = tap(2 - r, 2 - s).astype(BF16) if 0 <= s <= 2 else jnp.zeros((C, C), BF16)
                col = C * (4 * r + j)
                dst[C * o : C * o + C, col : col + C] = value


NN = (((1,), (0,)), ((), ()))
NT = (((1,), (1,)), ((), ()))
TN = (((0,), (0,)), ((), ()))


def dot(a, b, dims=NN):
    return lax.dot_general(a, b, dims, preferred_element_type=F32)


def rows_one(buf, i, q):
    return jnp.concatenate(
        [buf[i, r : r + 16, :, 256 * q : 256 * q + 512].reshape(256, 512) for r in range(3)], 1
    )


def rows_two(buf, first, number):
    return jnp.concatenate(
        [buf[pl.ds(first, number), r : r + 8].reshape(128 * number, 512) for r in range(3)], 1
    )


def by_two(count, work):
    odd = count % 2 == 1

    @pl.when(odd)
    def _():
        work(count - 1, 1, True)

    @pl.when(jnp.logical_not(odd))
    def _():
        work(0, 2, True)

    def step(p, _):
        work(2 * p, 2, False)
        return 0

    lax.fori_loop(jnp.where(odd, 0, 1), count // 2, step, 0)


def conv_all(count, work):
    def step(p, _):
        work(2 * p, 2)
        return 0

    loop(count // 2, step)

    @pl.when(count % 2 == 1)
    def _():
        work(count - 1, 1)


def conv_one(count, pairs, emit, dims=NN):
    def images(first, number):
        for n in range(number):
            for q in range(2):
                value = None
                for buf, weights in pairs:
                    term = dot(rows_one(buf, first + n, q), weights[...], dims)
                    value = term if value is None else value + term
                emit(first + n, q, value)

    conv_all(count, images)


def conv_two(count, pairs, dst, dims=NN):
    def images(first, number):
        value = None
        for buf, weights in pairs:
            term = dot(rows_two(buf, 2 * first, 2 * number), weights[...], dims)
            value = term if value is None else value + term
        dst[pl.ds(2 * first, 2 * number)] = value.reshape(2 * number, 8, 16, 256)

    conv_all((count + 1) // 2, images)


def kernel_grad_one(count, x, d, acc):
    def images(first, number, fresh):
        places = [(first + n, q) for n in range(number) for q in range(2)]
        grads = jnp.concatenate(
            [d[i, 1:17, :, 128 + 256 * q : 384 + 256 * q].reshape(256, 256) for i, q in places], 0
        )
        for r in range(3):
            ins = jnp.concatenate(
                [x[i, r : r + 16, :, 256 * q : 256 * q + 512].reshape(256, 512) for i, q in places],
                0,
            )
            value = dot(ins, grads, TN)
            acc[r] = value if fresh else acc[r] + value

    by_two(count, images)


def kernel_grad_two(count, pairs, acc):
    def images(first, number, fresh):
        at, size = pl.ds(2 * first, 2 * number), 256 * number
        grads = jnp.concatenate([d[at, 1:9, :, 128:384].reshape(size, 256) for _, d in pairs], 0)
        for r in range(3):
            ins = jnp.concatenate([x[at, r : r + 8].reshape(size, 512) for x, _ in pairs], 0)
            value = dot(ins, grads, TN)
            acc[r] = value if fresh else acc[r] + value

    by_two((count + 1) // 2, images)


def grad_tap(acc, r, s):
    return (
        acc[r, C * s : C * s + C, 0:C] + acc[r, C * (s + 1) : C * (s + 1) + C, C : 2 * C]
    )


def statistics(count, z, cells, tiles, chunk, blocks, summed=None):
    def add(i, acc):
        for start in range(0, tiles, chunk):
            for m in range(blocks):
                acc = acc + total(get(z, i, start, chunk, m))
        return acc

    zero = jnp.zeros((8, C), F32)
    mean = channel(loop(count, add, zero) if summed is None else summed) / cells

    def add_square(i, acc):
        for start in range(0, tiles, chunk):
            for m in range(blocks):
                centred = get(z, i, start, chunk, m) - mean
                set_(z, i, start, chunk, m, centred)
                acc = acc + total(centred * centred)
        return acc

    variance = channel(loop(count, add_square, zero)) / cells
    return lax.rsqrt(variance + EPSILON)


def activate(count, zc, s1, s2, pools, inverse, gain, shift, tiles, chunk, blocks, emit):
    scale, offset = 0.5 * gain * inverse, 0.5 * shift

    def step(i, _):
        for start in range(0, tiles, chunk):
            for half in range(blocks // 2):
                sums = []
                for m in (2 * half, 2 * half + 1):
                    centred = get(zc, i, start, chunk, m)
                    h = centred * scale + offset
                    bend = jnp.tanh(h)
                    over, under = 1.0 + bend, 1.0 - bend
                    slope = over * (1.0 + h * under)
                    set_(s1, i, start, chunk, m, slope)
                    if s2 is not None:
                        set_(s2, i, start, chunk, m, over * under * (1.0 - h * bend))
                    sums.append([jnp.sum(v, axis=1) for v in (h * over, slope, slope * centred)])
                pooled, *slopes = (one + two for one, two in zip(*sums))
                for ref, value in zip(pools, slopes):
                    place = i, slice(start // 2, start // 2 + chunk // 2), slice(None), slice(C * half, C * half + C)
                    ref[place] = value.reshape(chunk // 2, 16, C)
                emit(i, start, half, pooled)
        return 0

    loop(count, step)


def pooled_sums(count, pools, up, tiles, blocks):
    def add(i, carry):
        sums = list(carry)
        for half in range(blocks // 2):
            weight = up(i, 0, half, tiles).reshape(tiles // 2, 2, 8, C)
            for n, ref in enumerate(pools):
                value = ref[i, :, :, C * half : C * half + C].reshape(tiles // 2, 2, 8, C)
                sums[n] = sums[n] + total(weight * value)
        return tuple(sums)

    zero = jnp.zeros((8, C), F32)
    return tuple(channel(v) for v in loop(count, add, (zero, zero)))


def first_backward(count, zc, s1, pools, up, dst, gain, inverse, cells, tiles, chunk, blocks):
    one, two = pooled_sums(count, pools, up, tiles, blocks)
    two = two * inverse
    mean_one, mean_two = one / cells, two / cells
    scale = gain * inverse
    offset, tilt = scale * mean_one, scale * mean_two * inverse

    def step(i, _):
        for start in range(0, tiles, chunk):
            for m in range(blocks):
                dy = scale * up(i, start, m // 2, chunk) * get(s1, i, start, chunk, m)
                dz = dy - offset - get(zc, i, start, chunk, m) * tilt
                put(dst, i, start, tiles, m, blocks, dz.reshape(-1, 8, C))
        return 0

    loop(count, step)
    return mean_one, mean_two, one, two


def clear_odd(count, buffers):
    @pl.when(count % 2 == 1)
    def _():
        for buf in buffers:
            buf[count] = jnp.zeros(buf.shape[1:], buf.dtype)


def mix_taps(weight, src, dst):
    for g in range(0, C, MIX_ROWS):
        rows = slice(g, g + MIX_ROWS)
        values = [src(f, rows) for f in range(9)]
        for q in range(9):
            acc = weight(q, 0) * values[0]
            for f in range(1, 9):
                acc = acc + weight(q, f) * values[f]
            dst(q, rows, acc)


def transform(acc, kernel, outer, inner, taps, g_low, t_one, t_two, fast):
    for f in range(9):
        g_low[:, C * f : C * f + C] = grad_tap(acc, f // 3, f % 3).astype(BF16)
    t_one[...] = dot(inner[...].astype(BF16), g_low[...])

    def write(q, rows, value):
        t_two[q, rows, :] = value

    mix_taps(
        lambda q, f: taps[q, f], lambda f, rows: t_one[rows, C * f : C * f + C], write
    )
    turned = dot(t_two[...].reshape(9 * C, C).astype(BF16), outer[...].astype(BF16), NT)
    fast[...] = kernel[...] - STEP_RATE * turned.reshape(9, C, C)


def transform_back(acc, outer, inner, taps, g_low, t_one, t_two, d_low, e, w, payload, u):
    for q in range(9):
        grad = grad_tap(acc, q // 3, q % 3)
        payload[C * q : C * q + C, :] = grad
        d_low[C * q : C * q + C, :] = (-STEP_RATE * grad).astype(BF16)
    e[...] = dot(d_low[...], outer[...].astype(BF16)).reshape(9, C, C)
    payload[AT_OUTER:AT_INNER, :] = dot(
        d_low[...], t_two[...].reshape(9 * C, C).astype(BF16), TN
    )

    def write(f, rows, value):
        w[rows, C * f : C * f + C] = value

    mix_taps(lambda f, q: taps[q, f], lambda q, rows: e[q, rows, :], write)
    w_low = w[...].astype(BF16)
    payload[AT_INNER:AT_SMALL, :] = dot(w_low, g_low[...], NT)
    u[...] = dot(inner[...].astype(BF16), w_low, TN)
    sums = []
    for first in range(0, 9, 3):
        parts = [jnp.zeros((8, C), F32)] * 27
        for g in range(0, C, 8):
            ones = [t_one[g : g + 8, C * f : C * f + C] for f in range(9)]
            for n in range(27):
                if n % 9 == 0:
                    grad = e[first + n // 9, g : g + 8, :]
                parts[n] = parts[n] + grad * ones[n % 9]
        sums += parts
    sums = jnp.concatenate([jnp.sum(v, axis=0, keepdims=True) for v in sums], 0)
    sums = jnp.concatenate([jnp.sum(sums, axis=1, keepdims=True), jnp.zeros((7, 1), F32)], 0)
    spread = jnp.broadcast_to(sums, (88, C))
    row = lax.broadcasted_iota(jnp.int32, (88, C), 0)
    lane = lax.broadcasted_iota(jnp.int32, (88, C), 1)
    spread = jnp.where(row % 9 == lane, spread, 0.0)
    chosen = lax.broadcasted_iota(jnp.int32, (16, 88), 1) // 9 == lax.broadcasted_iota(
        jnp.int32, (16, 88), 0
    )
    payload[AT_SMALL : AT_SMALL + 16, :] = lax.dot_general(
        chosen.astype(F32), spread, NN, precision=lax.Precision.HIGHEST, preferred_element_type=F32
    )


def second_sums(count, c, zc, s1, up, inverse, cells, tiles, chunk, blocks):
    def add(i, carry):
        one, two, three = carry
        for start in range(0, tiles, chunk):
            for m in range(blocks):
                value = get(c, i, start, chunk, m)
                dy = up(i, start, m // 2, chunk) * get(s1, i, start, chunk, m)
                one = one + total(value)
                two = two + total(value * get(zc, i, start, chunk, m))
                three = three + total(value * dy)
        return one, two, three

    zero = jnp.zeros((8, C), F32)
    one, two, three = loop(count, add, (zero, zero, zero))
    return channel(one) / cells, channel(two) * inverse / cells, channel(three) / cells


def second_turn(count, c, zc, s1, s2, up, means, gain, inverse, emit, tiles, chunk, blocks):
    mean_c, mean_cz, _ = means
    scale, tilt = gain * inverse, mean_cz * inverse

    def step(i, carry):
        one, two = carry
        for start in range(0, tiles, chunk):
            for half in range(blocks // 2):
                pooled = None
                weight = scale * up(i, start, half, chunk)
                for m in (2 * half, 2 * half + 1):
                    centred = get(zc, i, start, chunk, m)
                    turned = get(c, i, start, chunk, m) - mean_c - centred * tilt
                    cy = turned * (weight * get(s2, i, start, chunk, m))
                    set_(s2, i, start, chunk, m, cy)
                    one = one + total(cy)
                    two = two + total(cy * centred)
                    if emit is not None:
                        part = jnp.sum(turned * get(s1, i, start, chunk, m), axis=1)
                        pooled = part if pooled is None else pooled + part
                if emit is not None:
                    emit(i, start, half, 0.5 * scale * pooled)
        return one, two

    zero = jnp.zeros((8, C), F32)
    one, two = loop(count, step, (zero, zero))
    return channel(one), channel(two) * inverse


def second_close(
    count, c, zc, s1, t_buf, up, extra, dst, means, sums, first_means, gain, inverse, cells, tiles, chunk, blocks
):
    mean_c, mean_cz, mean_cdy = means
    mean_dy, mean_dyz = first_means
    mean_cy, mean_cyz = sums[0] / cells, sums[1] / cells
    scale = gain * inverse
    mean_cw = mean_cdy - mean_c * mean_dy - mean_cz * mean_dyz
    mean_z = gain * mean_cy - scale * (mean_c * mean_dyz + mean_dy * mean_cz)
    mean_zz = gain * mean_cyz - 2.0 * scale * mean_cz * mean_dyz
    alpha = inverse * gain
    beta = scale * inverse * mean_dyz
    gamma = scale * inverse * mean_cz
    delta = inverse * mean_z
    epsilon = inverse * inverse * (mean_zz + scale * mean_cw)

    def step(i, _):
        for start in range(0, tiles, chunk):
            for m in range(blocks):
                weight = -gamma * up(i, start, m // 2, chunk)
                if extra is not None:
                    weight = weight + alpha * extra(i, start, m // 2, chunk)
                value = (
                    alpha * get(t_buf, i, start, chunk, m)
                    + weight * get(s1, i, start, chunk, m)
                    - beta * get(c, i, start, chunk, m)
                    - epsilon * get(zc, i, start, chunk, m)
                    - delta
                )
                put(dst, i, start, tiles, m, blocks, value.reshape(-1, 8, C))
        return 0

    loop(count, step)
    return sums[1] + inverse * cells * mean_cw


def image_grads(count, pairs, dst, wide):
    def emit(i, q, value):
        for o in range(2):
            v = value[:, C * o : C * o + C].reshape(16, 2, 8, C)
            for b in range(2):
                wide[16 * b : 16 * b + 16, pl.ds(2 * q + o, 8, stride=4), :] = v[:, b]
        if q == 1:
            dst[i] = wide[...].astype(BF16)

    conv_one(count, pairs, emit, NT)

    def dead(i, _):
        dst[i] = jnp.zeros(dst.shape[1:], BF16)
        return 0

    lax.fori_loop(count, dst.shape[0], dead, 0)


def query_grad_kernel(count, grads, weights, after, dst, zeros, wide):
    zeros[...] = jnp.zeros(zeros.shape, F32)
    image_grads(count[0], [(grads, weights)], dst, wide)


def support_grad_kernel(
    count, inner_grads, inner_weights, grads, kernel, after, dst, zeros, wide, weights
):
    zeros[...] = jnp.zeros(zeros.shape, F32)
    write_weights_back(weights, lambda r, s: kernel[3 * r + s])
    image_grads(count[0], [(inner_grads, inner_weights), (grads, weights)], dst, wide)


def run_image_grads(kernel, name, shape, after, operands, scratch):
    vmem = pl.BlockSpec(memory_space=pltpu.VMEM)
    images = operands[1].shape[0]
    convs = (len(operands) - 1) // 2
    return pl.pallas_call(
        kernel,
        out_shape=(jax.ShapeDtypeStruct(shape, BF16), pltpu.VMEM((8, C), F32)),
        in_specs=[pl.BlockSpec(memory_space=pltpu.SMEM)]
        + [vmem] * (len(operands) - 1)
        + [pl.BlockSpec(memory_space=pl.ANY)],
        out_specs=(vmem, vmem),
        scratch_shapes=[pltpu.VMEM((32, 32, C), F32)] + scratch,
        compiler_params=pltpu.CompilerParams(vmem_limit_bytes=VMEM_SMALL),
        cost_estimate=pl.CostEstimate(
            flops=2 * images * convs * 1024 * 1536 * C,
            bytes_accessed=images * (convs + 1) * 32 * 32 * C * 2,
            transcendentals=0,
        ),
        name=name,
    )(*operands, after)


SCALARS = ["support_count", "query_count", "taps_one", "taps_two"]
NORMS = ["gain_one", "shift_one", "gain_two", "shift_two"]
AT_OUTER, AT_INNER, AT_SMALL, AT_GAIN, HALF_ROWS = 9 * C, 10 * C, 11 * C, 11 * C + 16, 11 * C + 32
QUARTER = HALF_ROWS // 4
FETCHED = [
    "support",
    "kernel_one",
    "gain_one",
    "shift_one",
    "gain_two",
    "shift_two",
    "kernel_two",
    "target",
    "inner_two",
    "outer_two",
    "inner_one",
    "outer_one",
    "query",
    "cotangent",
]
HELD = ["query_output", "grad_q", "back_q", "grad_s", "back_s", "grad_e"]
KEPT = [f"keep_{at}" for at in range(4)]
GIVEN = [f"send_{at}" for at in range(4)]


def scratch_of(s_cap, q_cap):
    def operand(count, tiles, blocks):
        return pltpu.VMEM((count, tiles + 2, 16, C * (blocks + 2)), BF16)

    def plain(count, tiles, blocks):
        return pltpu.VMEM((count, tiles, 16, C * blocks), F32)

    weights = pltpu.VMEM((1536, 256), BF16)
    weights_back = pltpu.VMEM((256, 1536), BF16)
    square = pltpu.VMEM((C, 9 * C), F32)
    square_low = pltpu.VMEM((C, 9 * C), BF16)
    stack = pltpu.VMEM((9, C, C), F32)
    s_even, q_even = s_cap + s_cap % 2, q_cap + q_cap % 2
    return dict(
        wide=pltpu.VMEM((32, 32, C), F32),
        xs=operand(s_cap, 16, 4),
        xq=operand(q_cap, 16, 4),
        ds=operand(s_cap, 16, 4),
        dq=operand(q_cap, 16, 4),
        zs=plain(s_cap, 16, 4),
        s1s=plain(s_cap, 16, 4),
        s2s=plain(s_cap, 16, 4),
        zq=plain(q_cap, 16, 4),
        s1q=plain(q_cap, 16, 4),
        hs=operand(s_even, 8, 2),
        ds2=operand(s_even, 8, 2),
        hq=operand(q_even, 8, 2),
        dq2=operand(q_even, 8, 2),
        zs2=plain(s_even, 8, 2),
        s1s2=plain(s_even, 8, 2),
        s2s2=plain(s_even, 8, 2),
        dhs=plain(s_even, 8, 2),
        chs_back=plain(s_even, 8, 2),
        zq2=plain(q_even, 8, 2),
        s1q2=plain(q_even, 8, 2),
        dhq=plain(q_even, 8, 2),
        p1s=plain(s_cap, 8, 2),
        p2s=plain(s_cap, 8, 2),
        p1s2=plain(s_cap, 4, 1),
        p2s2=plain(s_cap, 4, 1),
        p1q=plain(q_cap, 8, 2),
        p2q=plain(q_cap, 8, 2),
        p1q2=plain(q_cap, 4, 1),
        p2q2=plain(q_cap, 4, 1),
        sums=pltpu.VMEM((3, 8, C), F32),
        w_a=weights,
        w_b=weights,
        w_c=weights,
        b_k2=weights_back,
        b_f1=weights_back,
        b_f2=weights_back,
        b_u1=weights_back,
        b_u2=weights_back,
        acc=pltpu.VMEM((3, 512, 256), F32),
        g_one=square_low,
        g_two=square_low,
        t1_one=square,
        t1_two=square,
        t2_one=stack,
        t2_two=stack,
        f_one=stack,
        f_two=stack,
        d_low=pltpu.VMEM((9 * C, C), BF16),
        e_buf=stack,
        w_buf=square,
        u_buf=square,
        payload=pltpu.VMEM((2, HALF_ROWS, C), F32),
        gain_one_v=pltpu.VMEM((1, C), F32),
        shift_one_v=pltpu.VMEM((1, C), F32),
        gain_two_v=pltpu.VMEM((1, C), F32),
        shift_two_v=pltpu.VMEM((1, C), F32),
        output_v=pltpu.VMEM((q_cap, 8, 8, C), BF16),
        support_v=pltpu.VMEM((s_cap, 32, 32, C), BF16),
        query_v=pltpu.VMEM((q_cap, 32, 32, C), BF16),
        target_v=pltpu.VMEM((s_cap, 8, 8, C), BF16),
        cotangent_v=pltpu.VMEM((q_cap, 8, 8, C), BF16),
        kernel_one_v=stack,
        kernel_two_v=stack,
        inner_one_v=pltpu.VMEM((C, C), F32),
        outer_one_v=pltpu.VMEM((C, C), F32),
        inner_two_v=pltpu.VMEM((C, C), F32),
        outer_two_v=pltpu.VMEM((C, C), F32),
        fetch_sem=pltpu.SemaphoreType.DMA((len(FETCHED),)),
        send_sem=pltpu.SemaphoreType.DMA((len(HELD),)),
    )


def task_kernel(names, *refs):
    k = SimpleNamespace(**dict(zip(names, refs)))
    fetches = {}
    for n, name in enumerate(FETCHED):
        fetches[name] = pltpu.make_async_copy(getattr(k, name), getattr(k, name + "_v"), k.fetch_sem.at[n])
        setattr(k, name, getattr(k, name + "_v"))
    for name in FETCHED[:6]:
        fetches[name].start()
    sent = []

    def ready(*wanted):
        for name in wanted:
            fetches[name].wait()

    def send(name, source):
        copy = pltpu.make_async_copy(source, getattr(k, name), k.send_sem.at[HELD.index(name)])
        copy.start()
        sent.append(copy)

    def close_layer(layer, gain_grad, shift_grad):
        pay = k.payload.at[layer]
        pay[AT_GAIN : AT_GAIN + 2, :] = jnp.concatenate([gain_grad[0:1], shift_grad[0:1]], 0)
        pay[AT_GAIN + 2 :, :] = jnp.zeros((HALF_ROWS - AT_GAIN - 2, C), F32)
        half, place = my_place()
        for at in range(4):
            rows = pl.ds(pl.multiple_of((place ^ at) * QUARTER, 8), QUARTER)
            for kept in (True, False):
                target = getattr(k, f"keep_{at}" if kept else f"send_{at}")

                @pl.when(half == (layer if kept else 1 - layer))
                def _(target=target, rows=rows):
                    target[...] = pay[rows, :]

    ns, nq = k.support_count[0], k.query_count[0]
    ns_f, nq_f = ns.astype(F32), nq.astype(F32)
    pay_one, pay_two = k.payload.at[0], k.payload.at[1]
    k.cs, k.es, k.cs2, k.es2, k.chs = k.zq, k.xq, k.zq2, k.hq, k.dq2
    one = dict(tiles=16, chunk=4, blocks=4)
    two = dict(tiles=8, chunk=4, blocks=2)
    wide = k.wide

    def load_images(count, src, dst):
        def image(i, _):
            wide[...] = src[i].astype(F32)
            for m in range(4):
                v = wide[:, pl.ds(m, 8, stride=4), :].reshape(2, 16, 1, 8, C)
                v = jnp.concatenate([v[0], v[1]], 1)
                put(dst, i, 0, 16, m, 4, v.reshape(32, 8, C))
            return 0

        loop(count, image)

    def keep(dst, terms):
        k.sums[...] = jnp.zeros(k.sums.shape, F32)

        def emit(i, q, value):
            dst[i, :, :, 256 * q : 256 * q + 256] = value.reshape(16, 16, 256)
            added = None
            for o in range(2):
                block = value[:, C * o : C * o + C].reshape(8, 2, 2, 8, C)
                parts = [total(term) for term in terms(i, 2 * q + o, block)]
                added = parts if added is None else [v + w for v, w in zip(added, parts)]
            for n, part in enumerate(added):
                k.sums[n] += part

        return emit

    def alone(i, m, block):
        return [block]

    def pool_to(dst):
        def emit(i, start, half, pooled):
            put(dst, i, start // 2, 8, half, 2, (0.25 * pooled).reshape(-1, 8, C))

        return emit

    def up_from(ref):
        def up(i, start, half, chunk):
            number = chunk // 2
            v = ref[i, start // 2 : start // 2 + number, :, C * half : C * half + C]
            return 0.125 * v.reshape(number, 1, 2, 8, C)

        return up

    def up_from_rows(ref, scale):
        def up(i, start, half, chunk):
            number = chunk // 2
            v = ref[i].astype(F32) * scale
            parts = [v[at : at + number].reshape(number, 1, 1, 8, C) for at in (start // 2, 4 + start // 2)]
            return jnp.concatenate(parts, 2)

        return up

    def tap_of(ref):
        return lambda r, s: ref[3 * r + s]

    def tap_wide(ref):
        return lambda r, s: ref[:, C * (3 * r + s) : C * (3 * r + s) + C]

    pools_one, pools_two = (k.p1s, k.p2s), (k.p1s2, k.p2s2)
    pools_q1, pools_q2 = (k.p1q, k.p2q), (k.p1q2, k.p2q2)

    cells_one, cells_two = ns_f * 1024.0, ns_f * 256.0
    ready("support")
    load_images(ns, k.support, k.xs)
    ready("kernel_one", *NORMS)
    write_weights(k.w_a, tap_of(k.kernel_one))
    for name in FETCHED[6:]:
        fetches[name].start()
    gain_one, shift_one, gain_two, shift_two = (
        jnp.broadcast_to(getattr(k, name)[...], (8, C)) for name in NORMS
    )
    conv_one(ns, [(k.xs, k.w_a)], keep(k.zs, alone))
    stats_one = statistics(ns, k.zs, cells_one, summed=k.sums[0], **one)
    activate(ns, k.zs, k.s1s, k.s2s, pools_one, stats_one, gain_one, shift_one, emit=pool_to(k.hs), **one)
    clear_odd(ns, [k.hs, k.ds2])
    ready("kernel_two", "target", "inner_two", "outer_two")
    write_weights(k.w_b, tap_of(k.kernel_two))
    conv_two(ns, [(k.hs, k.w_b)], k.zs2)
    stats_two = statistics(ns, k.zs2, cells_two, **two)
    activate(ns, k.zs2, k.s1s2, k.s2s2, pools_two, stats_two, gain_two, shift_two, emit=lambda *a: None, **two)

    up_two = up_from_rows(k.target, 1.0 / (512.0 * ns_f))
    mean_dy2, mean_dyz2, _, _ = first_backward(
        ns, k.zs2, k.s1s2, pools_two, up_two, k.ds2, gain_two, stats_two, cells_two, **two
    )
    kernel_grad_two(ns, [(k.hs, k.ds2)], k.acc)
    transform(
        k.acc, k.kernel_two, k.outer_two, k.inner_two, k.taps_two, k.g_two, k.t1_two, k.t2_two, k.f_two
    )
    write_weights_back(k.b_k2, tap_of(k.kernel_two))
    conv_two(ns, [(k.ds2, k.b_k2)], k.dhs, NT)
    up_one = up_from(k.dhs)
    mean_dy1, mean_dyz1, _, _ = first_backward(
        ns, k.zs, k.s1s, pools_one, up_one, k.ds, gain_one, stats_one, cells_one, **one
    )
    send("grad_s", k.ds)
    ready("inner_one", "outer_one", "query", "cotangent")
    kernel_grad_one(ns, k.xs, k.ds, k.acc)
    transform(
        k.acc, k.kernel_one, k.outer_one, k.inner_one, k.taps_one, k.g_one, k.t1_one, k.t2_one, k.f_one
    )

    cells_q1, cells_q2 = nq_f * 1024.0, nq_f * 256.0
    write_weights(k.w_a, tap_of(k.f_one))
    load_images(nq, k.query, k.xq)
    conv_one(nq, [(k.xq, k.w_a)], keep(k.zq, alone))
    stats_q1 = statistics(nq, k.zq, cells_q1, summed=k.sums[0], **one)
    activate(nq, k.zq, k.s1q, None, pools_q1, stats_q1, gain_one, shift_one, emit=pool_to(k.hq), **one)
    clear_odd(nq, [k.hq, k.dq2])
    write_weights(k.w_c, tap_of(k.f_two))
    conv_two(nq, [(k.hq, k.w_c)], k.zq2)
    stats_q2 = statistics(nq, k.zq2, cells_q2, **two)

    def produce(i, start, half, pooled):
        v = (0.25 * pooled).astype(BF16)
        at, number = start // 2, v.shape[0]
        k.output_v[i, at : at + number] = v[:, 0]
        k.output_v[i, 4 + at : 4 + at + number] = v[:, 1]

    activate(nq, k.zq2, k.s1q2, None, pools_q2, stats_q2, gain_two, shift_two, emit=produce, **two)

    def dead(i, _):
        k.output_v[i] = jnp.zeros(k.output_v.shape[1:], BF16)
        return 0

    lax.fori_loop(nq, k.output_v.shape[0], dead, 0)
    send("query_output", k.output_v)

    _, _, db2, dg2 = first_backward(
        nq, k.zq2, k.s1q2, pools_q2, up_from_rows(k.cotangent, 0.125 / nq_f), k.dq2, gain_two, stats_q2, cells_q2, **two
    )
    kernel_grad_two(nq, [(k.hq, k.dq2)], k.acc)
    transform_back(
        k.acc, k.outer_two, k.inner_two, k.taps_two, k.g_two, k.t1_two, k.t2_two, k.d_low, k.e_buf, k.w_buf,
        pay_two, k.u_buf,
    )
    write_weights_back(k.b_f2, tap_of(k.f_two))
    write_weights(k.w_c, tap_wide(k.u_buf))
    write_weights_back(k.b_u2, tap_wide(k.u_buf))
    conv_two(nq, [(k.dq2, k.b_f2)], k.dhq, NT)
    _, _, db1, dg1 = first_backward(
        nq, k.zq, k.s1q, pools_q1, up_from(k.dhq), k.dq, gain_one, stats_q1, cells_q1, **one
    )
    send("grad_q", k.dq)
    kernel_grad_one(nq, k.xq, k.dq, k.acc)
    transform_back(
        k.acc, k.outer_one, k.inner_one, k.taps_one, k.g_one, k.t1_one, k.t2_one, k.d_low, k.e_buf, k.w_buf,
        pay_one, k.u_buf,
    )
    write_weights_back(k.b_f1, tap_of(k.f_one))
    send("back_q", k.b_f1)
    write_weights(k.w_a, tap_wide(k.u_buf))
    write_weights_back(k.b_u1, tap_wide(k.u_buf))
    send("back_s", k.b_u1)

    clear_odd(ns, [k.chs, k.es2])

    def second_terms(i, m, block):
        dy = up_one(i, 0, m // 2, 16) * get(k.s1s, i, 0, 16, m)
        return [block, block * get(k.zs, i, 0, 16, m), block * dy]

    conv_one(ns, [(k.xs, k.w_a)], keep(k.cs, second_terms))
    means_one = tuple(channel(k.sums[n]) / cells_one for n in range(3))
    means_one = means_one[0], means_one[1] * stats_one, means_one[2]
    turn_one = second_turn(
        ns, k.cs, k.zs, k.s1s, k.s2s, up_one, means_one, gain_one, stats_one, pool_to(k.chs), **one
    )
    conv_two(ns, [(k.chs, k.w_b), (k.hs, k.w_c)], k.cs2)
    means_two = second_sums(ns, k.cs2, k.zs2, k.s1s2, up_two, stats_two, cells_two, **two)
    turn_two = second_turn(
        ns, k.cs2, k.zs2, k.s1s2, k.s2s2, up_two, means_two, gain_two, stats_two, None, **two
    )
    extra_g2 = second_close(
        ns, k.cs2, k.zs2, k.s1s2, k.s2s2, up_two, None, k.es2, means_two, turn_two, (mean_dy2, mean_dyz2),
        gain_two, stats_two, cells_two, **two,
    )
    conv_two(ns, [(k.ds2, k.b_u2), (k.es2, k.b_k2)], k.chs_back, NT)
    kernel_grad_two(ns, [(k.chs, k.ds2), (k.hs, k.es2)], k.acc)
    for f in range(9):
        pay_two[C * f : C * f + C, :] += grad_tap(k.acc, f // 3, f % 3)
    close_layer(1, dg2 + extra_g2, db2 + turn_two[0])
    up_back = up_from(k.chs_back)
    more = pooled_sums(ns, pools_one, up_back, 16, 4)
    turn_one = (turn_one[0] + more[0], turn_one[1] + more[1] * stats_one)
    extra_g1 = second_close(
        ns, k.cs, k.zs, k.s1s, k.s2s, up_one, up_back, k.es, means_one, turn_one, (mean_dy1, mean_dyz1),
        gain_one, stats_one, cells_one, **one,
    )
    send("grad_e", k.es.at[pl.ds(0, k.xs.shape[0])])
    kernel_grad_one(ns, k.xs, k.es, k.acc)
    for f in range(9):
        pay_one[C * f : C * f + C, :] += grad_tap(k.acc, f // 3, f % 3)
    close_layer(0, dg1 + extra_g1, db1 + turn_one[0])
    for copy in sent:
        copy.wait()


def run_task(values):
    s_cap, q_cap = values["support"].shape[0], values["query"].shape[0]
    scratch = scratch_of(s_cap, q_cap)
    vmem = pl.BlockSpec(memory_space=pltpu.VMEM)
    smem = pl.BlockSpec(memory_space=pltpu.SMEM)
    anywhere = pl.BlockSpec(memory_space=pl.ANY)

    def operand(count):
        return jax.ShapeDtypeStruct((count, 18, 16, 6 * C), BF16)

    back = jax.ShapeDtypeStruct((256, 1536), BF16)
    rows = pltpu.VMEM((QUARTER, C), F32)
    inputs = SCALARS + FETCHED
    outputs = HELD + KEPT + GIVEN
    results = pl.pallas_call(
        partial(task_kernel, inputs + outputs + list(scratch)),
        out_shape=(
            jax.ShapeDtypeStruct(values["cotangent"].shape, BF16),
            operand(q_cap),
            back,
            operand(s_cap),
            back,
            operand(s_cap),
            *[rows] * 8,
        ),
        in_specs=[smem] * len(SCALARS) + [anywhere] * len(FETCHED),
        out_specs=[anywhere] * len(HELD) + [vmem] * 8,
        scratch_shapes=list(scratch.values()),
        compiler_params=pltpu.CompilerParams(vmem_limit_bytes=VMEM_BYTES),
        name="task",
    )(*[values[name] for name in inputs])
    return dict(zip(outputs, results))


def swap(value, mask):
    extent = lax.axis_size(AXES)
    return lax.ppermute(value, AXES, [(place, place ^ mask) for place in range(extent)])


def sum_quarters(kept, sent, first, second):
    extent = lax.axis_size(AXES)
    come = {n: swap(sent[n], 1) for n in (3, 1, 2, 0)}
    mine = {n: kept[n] + come[n] for n in (3, 1, 2, 0)}
    terms = {n: swap(mine[n], 2 * n) for n in (3, 1, 2)}
    one, zeros = first(come[0][0:8])
    part = mine[0] + terms[3] + terms[1] + terms[2] + zeros[0:1]
    mask, two = 8, None
    while mask < extent:
        passed = swap(part, mask)
        if 2 * mask >= extent:
            two, zeros = second(part[0:8])
            passed = passed + zeros[0:1]
        part = part + passed
        mask *= 2
    if two is None:
        two, _ = second(part[0:8])
    quarters = [part] + [swap(part, 2 * n) for n in (1, 2, 3)]
    return one, two, quarters, [swap(quarter, 1) for quarter in quarters]


def sum_plain(kept, sent, first, second):
    half, at = my_place()
    whole = jnp.stack([*kept, *sent]).reshape(2, 4, QUARTER, C)
    whole = jnp.where(half == 0, whole, whole[::-1])
    order = at ^ jnp.arange(4)
    whole = lax.psum(jnp.take(whole, order, axis=1), AXES)
    whole = jnp.take(jnp.where(half == 0, whole, whole[::-1]), order, axis=1)
    results = first(whole)[0], second(whole)[0]
    return *results, list(whole[0]), list(whole[1])


LAYER = ["outer", "inner", "taps"]


def my_place():
    me = lax.axis_index(AXES)
    return me & 1, (me >> 1) & 3


def finish_kernel(*refs):
    pieces, refs = refs[:8], refs[8:]
    factors, refs = refs[:6], refs[6:]
    results, refs = refs[:12], refs[12:]
    rest, kernel_sem = refs
    half, at = my_place()
    whole = AT_OUTER // QUARTER
    last = AT_OUTER - whole * QUARTER
    for n, piece in enumerate(pieces):
        quarter = at ^ (n % 4)
        for layer in range(2):
            kernel = results[6 * layer]
            own = half == layer if n < 4 else half != layer

            @pl.when(own & (quarter < whole))
            def _(piece=piece, kernel=kernel, quarter=quarter, layer=layer):
                start = pl.multiple_of(quarter * QUARTER, 8)
                pltpu.make_async_copy(
                    piece, kernel.at[pl.ds(start, QUARTER)], kernel_sem.at[layer]
                ).start()

            @pl.when(own & (quarter == whole))
            def _(piece=piece, kernel=kernel, layer=layer):
                rest[layer] = piece[last:QUARTER, :]
                pltpu.make_async_copy(
                    piece.at[pl.ds(0, last)], kernel.at[pl.ds(whole * QUARTER, last)], kernel_sem.at[layer]
                ).start()

    for layer in range(2):
        kernel, gain, shift, outer, inner, taps = results[6 * layer : 6 * layer + 6]
        base = AT_GAIN - AT_OUTER
        gain[...] = rest[layer, base : base + 1, :]
        shift[...] = rest[layer, base + 1 : base + 2, :]
        for start, size, factor, result in zip(
            (0, C, 2 * C), (C, C, 9), factors[3 * layer : 3 * layer + 3], (outer, inner, taps)
        ):
            row = lax.broadcasted_iota(jnp.int32, (size, size), 0)
            column = lax.broadcasted_iota(jnp.int32, (size, size), 1)
            unit = jnp.where(row == column, 1.0, 0.0)
            value = rest[layer, start : start + size, :size]
            result[...] = value + 2.0 * PENALTY * (factor[...] - unit)
    for layer in range(2):
        kernel = results[6 * layer]
        pltpu.make_async_copy(kernel, kernel, kernel_sem.at[layer]).wait()


def run_finish(pieces, factors):
    vmem = pl.BlockSpec(memory_space=pltpu.VMEM)
    anywhere = pl.BlockSpec(memory_space=pl.ANY)

    def shape(*dims):
        return jax.ShapeDtypeStruct(dims, F32)

    layer = [shape(9 * C, C), shape(1, C), shape(1, C), shape(C, C), shape(C, C), shape(9, 9)]
    return pl.pallas_call(
        finish_kernel,
        out_shape=layer * 2,
        in_specs=[vmem] * 14,
        out_specs=([anywhere] + [vmem] * 5) * 2,
        scratch_shapes=[
            pltpu.VMEM((2, HALF_ROWS - AT_OUTER, C), F32),
            pltpu.SemaphoreType.DMA((2,)),
        ],
        compiler_params=pltpu.CompilerParams(vmem_limit_bytes=VMEM_SMALL),
        name="finish",
    )(*pieces, *factors)


def body(
    support_images,
    query_images,
    support_target,
    query_cotangent,
    support_count,
    query_count,
    kernel_one,
    kernel_two,
    gain_one,
    shift_one,
    gain_two,
    shift_two,
    outer_one,
    inner_one,
    taps_one,
    outer_two,
    inner_two,
    taps_two,
):
    shared = dict(
        taps_one=taps_one,
        taps_two=taps_two,
        kernel_one=kernel_one.reshape(9, C, C),
        kernel_two=kernel_two.reshape(9, C, C),
        gain_one=gain_one.reshape(1, C),
        shift_one=shift_one.reshape(1, C),
        gain_two=gain_two.reshape(1, C),
        shift_two=shift_two.reshape(1, C),
        outer_one=outer_one,
        inner_one=inner_one,
        outer_two=outer_two,
        inner_two=inner_two,
    )
    tasks = range(support_images.shape[0])
    results = [
        run_task(
            dict(
                shared,
                support_count=support_count[task : task + 1],
                query_count=query_count[task : task + 1],
                support=support_images[task],
                query=query_images[task],
                target=support_target[task],
                cotangent=query_cotangent[task],
            )
        )
        for task in tasks
    ]

    def query_grads(after):
        done = [
            run_image_grads(
                query_grad_kernel,
                "query_grad",
                query_images.shape[1:],
                after,
                [query_count[task : task + 1], results[task]["grad_q"], results[task]["back_q"]],
                [],
            )
            for task in tasks
        ]
        return jnp.stack([value for value, _ in done]), sum(zeros for _, zeros in done)

    def support_grads(after):
        done = [
            run_image_grads(
                support_grad_kernel,
                "support_grad",
                support_images.shape[1:],
                after,
                [
                    support_count[task : task + 1],
                    *[results[task][name] for name in ("grad_s", "back_s", "grad_e")],
                    shared["kernel_one"],
                ],
                [pltpu.VMEM((256, 1536), BF16)],
            )
            for task in tasks
        ]
        return jnp.stack([value for value, _ in done]), sum(zeros for _, zeros in done)

    kept = [sum(result[name] for result in results) for name in KEPT]
    sent = [sum(result[name] for result in results) for name in GIVEN]
    extent = lax.axis_size(AXES)
    if extent < 8 or extent & (extent - 1):
        summed = sum_plain(kept, sent, query_grads, support_grads)
    else:
        summed = sum_quarters(kept, sent, query_grads, support_grads)
    query_grad, support_grad, mine, others = summed
    factors = [outer_one, inner_one, taps_one, outer_two, inner_two, taps_two]
    last = run_finish([*mine, *others], factors)
    return (
        jnp.stack([result["query_output"] for result in results]),
        support_grad,
        query_grad,
        last[0].reshape(3, 3, C, C),
        last[6].reshape(3, 3, C, C),
        *[last[at].reshape(C) for at in (1, 2, 7, 8)],
        *last[3:6],
        *last[9:12],
    )


def solution(mesh):
    split = P(("tasks", "group"))
    return jax.shard_map(
        body,
        mesh=mesh,
        in_specs=(split,) * 6 + (P(),) * 12,
        out_specs=(split,) * 3 + (P(),) * 12,
        check_vma=False,
    )
```
